128 devices in a mesh: row: 8 (over x, core), col: 16 (over z, y).
Axes of the slice: x: 4, y: 4, z: 4, core: 2. Of those that a mesh axis runs over, the one named last changes fastest.
Arguments:
- object_field: float32 [2, 4096, 8192], P(None, 'row', 'col'), may hold values from -5 to 5
- probe: float32 [4, 2, 256, 256], replicated, may hold values from -4 to 4
- measured: float32 [384, 256, 256], P(('row', 'col')), may hold values from 0.2 to 4
- offsets: int32 [128, 2], replicated, may hold values from 0 to 7936, as said below
- owner: int32 [128], replicated, may hold values from 0 to 15, as said below
Outputs:
- new_object: float32 [2, 4096, 8192], P(None, 'row', 'col')
- new_probe: float32 [4, 2, 256, 256], replicated
The draws below stay inside these ranges and needn't reach their ends.
Inputs may be any that keep to these rules, and one draw needn't show every extreme that they name: `offsets`: position p's patch corner lies in the tile of device p (numbered row-major over row, col; tiles of 512 x 512 pixels), and the whole 256 x 256 patch lies inside the object. owner[p] names a device in the same mesh row as p's tile. Each device holds at most 3 positions' measurements in its first slots, in order of position; in every mesh row one device holds exactly 3. Other slots are unused.
All inputs are finite; a program needn't handle non-finite values.
Results may differ from the reference program's by a relative error of at most 0.0001.
Values sent between devices are 32-bit elements; how exact they have to be, the bound alone decides.
No kernel may reach another device: no remote copies, remote signals or barrier semaphores. Data moves between devices by JAX's collectives and lax.ppermute only.
A program may use at most 128 MiB of HBM per device.

```python
import jax
import jax.numpy as jnp
from jax import lax

W = 256
MODES = 4
TILE = 512
POS_DEV = 1
CAP = 3
POSITIONS = 128
NY = 4096
NX = 8192
N_ROW = 8
N_COL = 16
DEVICES = 128


def draw_offsets(key, part):
    key = jax.random.fold_in(key, 11)
    first_key, second_key = jax.random.split(key)
    place = jnp.arange(POSITIONS) // POS_DEV
    tile_row = place // N_COL
    tile_col = place % N_COL
    high_row = jnp.where(tile_row == N_ROW - 1, TILE - W + 1, TILE)
    high_col = jnp.where(tile_col == N_COL - 1, TILE - W + 1, TILE)
    local_row = jax.random.randint(first_key, (POSITIONS,), 0, high_row)
    local_col = jax.random.randint(second_key, (POSITIONS,), 0, high_col)
    local_row = local_row.at[0].set(0).at[POSITIONS - 1].set(TILE - W)
    local_col = local_col.at[0].set(0).at[POSITIONS - 1].set(TILE - W)
    return jnp.stack([tile_row * TILE + local_row, tile_col * TILE + local_col], axis=1).astype(jnp.int32)


def draw_owner(key, part):
    key = jax.random.fold_in(key, 23)
    per_row = N_COL * POS_DEV

    def one_row(row_key, row_number):
        key_a, key_b, key_c = jax.random.split(row_key, 3)
        order = jax.random.permutation(key_a, per_row)
        picked = jax.random.randint(key_b, (), 0, N_COL)
        busiest = jnp.where(row_number == 0, N_COL - 1, jnp.where(row_number == 1, 0, picked))
        others = (busiest + 1 + jax.random.permutation(key_c, N_COL - 1)) % N_COL
        index = jnp.arange(per_row)
        columns = jnp.where(index < CAP, busiest, others[jnp.maximum(index - CAP, 0) % (N_COL - 1)])
        return jnp.zeros((per_row,), jnp.int32).at[order].set(columns.astype(jnp.int32))
    keys = jax.random.split(key, N_ROW)
    return jax.vmap(one_row)(keys, jnp.arange(N_ROW)).reshape(-1).astype(jnp.int32)


def block_levels(own_key, dims, cuts, least, top_value):
    gain = 1.0
    for dim, shards_of in cuts:
        steps = jax.random.uniform(jax.random.fold_in(jax.random.fold_in(own_key, 6), dim), (shards_of,), jnp.float32, least / len(cuts), top_value / len(cuts))
        gain = gain * jnp.repeat(jnp.exp(steps), dims[dim] // shards_of).reshape((-1,) + (1,) * (len(dims) - 1 - dim))
    return gain


def centred(own_key, shape, spread, limit, pieces=(), kind=jnp.bfloat16):
    drawn = jax.random.normal(own_key, shape, jnp.float32) * spread
    if len(pieces) > 0:
        drawn = block_levels(own_key, shape, pieces, -0.22, 0.18) * drawn
    return jnp.clip(drawn, min=-limit, max=limit).astype(kind)


def setup_inputs(seed: int = 0) -> dict:
    arg_keys = jax.random.split(jax.random.key(seed), 6)
    object_field = centred(arg_keys[0], (2, NY, NX), 0.7, 5.0, ((1, 8), (2, 16)), jnp.float32)
    probe = centred(arg_keys[1], (MODES, 2, W, W), 0.5, 4.0, (), jnp.float32)
    measured = jnp.clip(0.2 + 3.8 * jax.random.uniform(arg_keys[2], (DEVICES * CAP, W, W), jnp.float32) ** block_levels(arg_keys[2], (DEVICES * CAP, W, W), ((0, 128),), -0.2, 0.2), 0.2, 4.0)
    offsets = draw_offsets(jax.random.fold_in(arg_keys[5], 71), 0)
    owner = draw_owner(jax.random.fold_in(arg_keys[5], 71), 0)
    return {"object_field": object_field, "probe": probe, "measured": measured, "offsets": offsets, "owner": owner}


def reference(object_field, probe, measured, offsets, owner):
    per_row = N_COL * POS_DEV
    grid = owner.reshape(N_ROW, per_row)
    same = grid[:, :, None] == grid[:, None, :]
    index = jnp.arange(per_row)
    earlier = index[None, :] < index[:, None]
    rank = lax.optimization_barrier(jnp.sum(jnp.logical_and(same, earlier[None]), axis=2)).reshape(-1).astype(jnp.int32)
    rows = (jnp.arange(POSITIONS) // per_row).astype(jnp.int32)
    slot = ((rows * N_COL + owner) * CAP + rank).astype(jnp.int32)
    amps_all = measured[slot]
    modes = probe[:, 0] + 1j * probe[:, 1]

    def step(carry, item):
        grad_re, grad_im, probe_re, probe_im = carry
        spot, amp = item
        patch_re = lax.dynamic_slice(object_field[0], (spot[0], spot[1]), (W, W))
        patch_im = lax.dynamic_slice(object_field[1], (spot[0], spot[1]), (W, W))
        patch = patch_re + 1j * patch_im
        far = jnp.fft.fft2(modes * patch[None], norm='ortho')
        inten = lax.optimization_barrier(jnp.sum(jnp.real(far) ** 2 + jnp.imag(far) ** 2, axis=0))
        factor = amp / jnp.maximum(jnp.sqrt(inten), 0.5) - 1.0
        back = jnp.fft.ifft2(far * factor[None], norm='ortho')
        local = lax.optimization_barrier(jnp.sum(jnp.conj(modes) * back, axis=0))
        pgrad = jnp.conj(patch)[None] * back
        old_re = lax.dynamic_slice(grad_re, (spot[0], spot[1]), (W, W))
        old_im = lax.dynamic_slice(grad_im, (spot[0], spot[1]), (W, W))
        grad_re = lax.dynamic_update_slice(grad_re, old_re + jnp.real(local), (spot[0], spot[1]))
        grad_im = lax.dynamic_update_slice(grad_im, old_im + jnp.imag(local), (spot[0], spot[1]))
        return ((grad_re, grad_im, probe_re + jnp.real(pgrad), probe_im + jnp.imag(pgrad)), None)
    start = (jnp.zeros_like(object_field[0]), jnp.zeros_like(object_field[1]), jnp.zeros_like(probe[:, 0]), jnp.zeros_like(probe[:, 1]))
    (grad_re, grad_im, probe_re, probe_im), _ = lax.scan(step, start, (offsets, amps_all))
    scale = 1.0 / (jnp.max(lax.optimization_barrier(jnp.sum(probe * probe, axis=(0, 1)))) + 1e-05)
    new_object = object_field + jnp.stack([grad_re, grad_im]) * scale
    new_probe = probe + jnp.stack([probe_re, probe_im], axis=1) / POSITIONS
    return (new_object, new_probe)
```

```python
import functools
import math

import jax
import jax.numpy as jnp
import ml_dtypes
import numpy as np
from jax import lax
from jax.experimental import pallas as pl
from jax.experimental.pallas import tpu as pltpu
from jax.sharding import Mesh
from jax.sharding import PartitionSpec as P

W = 256
HALF = 128
TILE = 512
MODES = 4
CAP = 3
NR = 8
NC = 16
ALL = ("x", "core", "z", "y")
COL = ("z", "y")
CHIPS = ("x", "z", "y")
CHUNK = W // NC
BF = jnp.bfloat16
F32 = jnp.float32


def dft_tables():
    n = np.arange(HALF)[:, None]
    q = np.arange(HALF)[None, :]
    out = []
    for k in (2 * q, 2 * q + 1):
        angle = 2.0 * math.pi * ((n * k) % W) / W
        c = np.cos(angle) / math.sqrt(W)
        s = np.sin(angle) / math.sqrt(W)
        m = np.block([[c, -s], [s, c]])
        for t in (m, m.T):
            hi = t.astype(ml_dtypes.bfloat16)
            lo = (t - hi.astype(np.float64)).astype(ml_dtypes.bfloat16)
            out += [hi, lo]
    order = np.concatenate([np.arange(0, W, 2), np.arange(1, W, 2)])
    perm = np.zeros((W, W))
    perm[np.arange(W), order] = 1.0
    out += [perm.astype(ml_dtypes.bfloat16), perm.T.astype(ml_dtypes.bfloat16)]
    return np.stack(out)


def routes():
    up, down, side_in, side_out, swap = [], [], [], [], []
    for r in range(NR):
        for c in range(NC):
            me = r * NC + c
            if r > 0:
                up.append((me, me - NC))
                down.append((me - NC, me))
            if r % 2 == 0:
                other = r * NC + (c - 1) % NC
            else:
                other = r * NC + (c + 1) % NC
            side_in.append((me, other))
            side_out.append((other, me))
            swap.append((me, (r ^ 1) * NC + c))
    return up, down, side_in, side_out, swap


UP, DOWN, SIDE_IN, SIDE_OUT, SWAP = routes()


def coords():
    core = lax.axis_index("core")
    row = lax.axis_index("x") * 2 + core
    col = lax.axis_index("z") * 4 + lax.axis_index("y")
    return row, col, core


def corner(offs, row, col):
    row = (row + NR) % NR
    col = (col + NC) % NC
    p = row * NC + col
    return offs[p, 0] - row * TILE, offs[p, 1] - col * TILE


def iota(shape, dim):
    return lax.broadcasted_iota(jnp.int32, shape, dim)


def send_up_kernel(offs, tile, first, second):
    row, col, core = coords()
    _, c = corner(offs, row - 1, col)
    b = iota((W, W), 1)
    c1 = jnp.where(core == 1, 0, c)
    c2 = jnp.where(core == 1, c, 0)
    for i in range(2):
        left = tile[i, :, :W]
        right = tile[i, :, W:]
        first[i] = jnp.where(b >= c1, left, right)
        second[i] = jnp.where(b >= c2, left, right)


def send_side_kernel(offs, tile, below, out):
    row, col, core = coords()
    _, c = corner(offs, row, col)
    r, _ = corner(offs, row, jnp.where(core == 0, col - 1, col))
    c = jnp.where(core == 0, 0, c)
    a = iota((W, W), 0)
    b = iota((W, W), 1)
    for i in range(2):
        top = jnp.where(b >= c, tile[i, :W, :W], tile[i, :W, W:])
        low = jnp.where(b >= c, tile[i, W:, :W], tile[i, W:, W:])
        out[i] = jnp.where(a >= r, top, jnp.where(a + W >= r, low, below[i]))


def split(x):
    hi = x.astype(BF)
    lo = (x - hi.astype(F32)).astype(BF)
    return hi, lo


def mm(a, b):
    return jnp.dot(a, b, preferred_element_type=F32)


def right(x, hi, lo):
    xh, xl = split(x)
    return mm(xh, hi) + mm(xh, lo) + mm(xl, hi)


def left(hi, lo, x):
    xh, xl = split(x)
    return mm(hi, xh) + mm(lo, xh) + mm(hi, xl)


def forward_kernel(offs, tile, below, side, probe, tables, far, mag, patch, scale):
    row, col, core = coords()
    r, c = corner(offs, row, jnp.where(core == 0, col, col - 1))
    c_own = jnp.where(core == 0, c, 0)
    a = iota((W, W), 0)
    b = iota((W, W), 1)
    beyond = jnp.where(c > b + W, 1, 0)
    use_side = beyond != core
    row_shift = (2 * W - r) % W
    col_shift = (2 * W - c) % W
    for i in range(2):
        top = jnp.where(b >= c_own, tile[i, :W, :W], tile[i, :W, W:])
        low = jnp.where(b >= c_own, tile[i, W:, :W], tile[i, W:, W:])
        own = jnp.where(a >= r, top, jnp.where(a + W >= r, low, below[i]))
        whole = jnp.where(use_side, side[i], own)
        patch[i] = pltpu.roll(pltpu.roll(whole, row_shift, 0), col_shift, 1)
    mag[...] = jnp.zeros((W, W), F32)
    scale[...] = jnp.zeros_like(scale)

    def mode(m, power):
        p_re = probe[m, 0]
        p_im = probe[m, 1]
        o_re = patch[0]
        o_im = patch[1]
        e_re = p_re * o_re - p_im * o_im
        e_im = p_re * o_im + p_im * o_re
        sums = jnp.concatenate([e_re[:, :HALF] + e_re[:, HALF:], e_im[:, :HALF] + e_im[:, HALF:]], axis=1)
        diff = jnp.concatenate([e_re[:, :HALF] - e_re[:, HALF:], e_im[:, :HALF] - e_im[:, HALF:]], axis=1)
        even = right(sums, tables[0], tables[1])
        odd = right(diff, tables[4], tables[5])
        h_re = jnp.concatenate([even[:, :HALF], odd[:, :HALF]], axis=1)
        h_im = jnp.concatenate([even[:, HALF:], odd[:, HALF:]], axis=1)
        sums = jnp.concatenate([h_re[:HALF] + h_re[HALF:], h_im[:HALF] + h_im[HALF:]], axis=0)
        diff = jnp.concatenate([h_re[:HALF] - h_re[HALF:], h_im[:HALF] - h_im[HALF:]], axis=0)
        even = left(tables[2], tables[3], sums)
        odd = left(tables[6], tables[7], diff)
        far[m, 0] = even
        far[m, 1] = odd
        mag[:HALF] += even[:HALF] * even[:HALF] + even[HALF:] * even[HALF:]
        mag[HALF:] += odd[:HALF] * odd[:HALF] + odd[HALF:] * odd[HALF:]
        return power + (p_re * p_re + p_im * p_im)

    power = lax.fori_loop(0, MODES, mode, jnp.zeros((W, W), F32))
    scale[...] = jnp.full(scale.shape, 1.0 / (jnp.max(power) + 1e-05), F32)


def backward_kernel(offs, far, mag, amp, patch, probe, tables, grad, give, keep, factor):
    row, col, core = coords()
    r, c = corner(offs, row, jnp.where(core == 0, col, col - 1))
    x = amp[...]
    perm = tables[8]
    perm_t = tables[9]
    for side in range(2):
        p1 = x.astype(BF)
        rest = x - p1.astype(F32)
        p2 = rest.astype(BF)
        p3 = (rest - p2.astype(F32)).astype(BF)
        if side == 0:
            x = mm(perm, p1) + mm(perm, p2) + mm(perm, p3)
        else:
            x = mm(p1, perm_t) + mm(p2, perm_t) + mm(p3, perm_t)
    factor[...] = x / jnp.maximum(jnp.sqrt(mag[...]), 0.5) - 1.0
    grad[...] = jnp.zeros_like(grad)

    def mode(t, carry):
        m = (t + 2 * (1 - core)) % MODES
        f_even = factor[:HALF]
        f_odd = factor[HALF:]
        even = far[m, 0] * jnp.concatenate([f_even, f_even], axis=0)
        odd = far[m, 1] * jnp.concatenate([f_odd, f_odd], axis=0)
        u = left(tables[0], tables[1], even)
        v = left(tables[4], tables[5], odd)
        h_re = jnp.concatenate([u[:HALF] + v[:HALF], u[:HALF] - v[:HALF]], axis=0)
        h_im = jnp.concatenate([u[HALF:] + v[HALF:], u[HALF:] - v[HALF:]], axis=0)
        u = right(jnp.concatenate([h_re[:, :HALF], h_im[:, :HALF]], axis=1), tables[2], tables[3])
        v = right(jnp.concatenate([h_re[:, HALF:], h_im[:, HALF:]], axis=1), tables[6], tables[7])
        b_re = jnp.concatenate([u[:, :HALF] + v[:, :HALF], u[:, :HALF] - v[:, :HALF]], axis=1)
        b_im = jnp.concatenate([u[:, HALF:] + v[:, HALF:], u[:, HALF:] - v[:, HALF:]], axis=1)
        p_re = probe[m, 0]
        p_im = probe[m, 1]
        o_re = patch[0]
        o_im = patch[1]
        grad[0] += p_re * b_re + p_im * b_im
        grad[1] += p_re * b_im - p_im * b_re
        g_re = o_re * b_re + o_im * b_im
        g_im = o_re * b_im - o_im * b_re

        @pl.when(t < 2)
        def _():
            give[t, 0] = g_re
            give[t, 1] = g_im

        @pl.when(t >= 2)
        def _():
            keep[t - 2, 0] = g_re
            keep[t - 2, 1] = g_im

        return carry

    lax.fori_loop(0, MODES, mode, 0)
    for i in range(2):
        grad[i] = pltpu.roll(pltpu.roll(grad[i], r % W, 0), c % W, 1)


def pick_kernel(owner, slots, out):
    row, col, core = coords()
    base = row * NC
    owners = [owner[base + i] for i in range(NC)]
    index = []
    for i in range(NC):
        rank = jnp.int32(0)
        for q in range(i):
            rank = rank + jnp.where(owners[q] == owners[i], 1, 0)
        index.append(owners[i] * CAP + rank)
    for i in range(NC):
        device = jnp.where(core == 0, i, (i + 1) % NC)
        out[device] = slots[index[i]]


def object_kernel(offs, tile, own, got, above_first, above_second, scale, out):
    row, col, core = coords()
    a = iota((W, W), 0)
    b = iota((W, W), 1)
    s = scale[0, 0]
    r_s, c_s = corner(offs, row, col)
    r_b, c_b = corner(offs, row, col - 1)
    r_as, c_as = corner(offs, row - 1, col)
    r_ab, c_ab = corner(offs, row - 1, col - 1)

    def bands(at, v):
        return [v <= at, jnp.logical_and(v > at, v <= at + W)]

    even = core == 0
    rows_s, cols_s = bands(a, r_s), bands(b, c_s)
    rows_b = bands(a, r_b)
    in_b = c_b > b + W
    cols_as = bands(b, c_as)
    low_as = r_as > a + W
    low_ab = jnp.logical_and(r_ab > a + W, c_ab > b + W)
    for i in range(2):
        g_s = jnp.where(even, own[i], got[i])
        g_b = jnp.where(even, got[i], own[i])
        d_s = jnp.where(even, above_second[i], above_first[i])
        d_b = jnp.where(even, above_first[i], above_second[i])
        for p in range(2):
            for q in range(2):
                total = jnp.where(jnp.logical_and(rows_s[p], cols_s[q]), g_s, 0.0)
                if q == 0:
                    total += jnp.where(jnp.logical_and(rows_b[p], in_b), g_b, 0.0)
                if p == 0:
                    total += jnp.where(jnp.logical_and(low_as, cols_as[q]), d_s, 0.0)
                if p == 0 and q == 0:
                    total += jnp.where(low_ab, d_b, 0.0)
                at = (i, pl.ds(p * W, W), pl.ds(q * W, W))
                out[at] = tile[at] + total * s


SMEM = pl.BlockSpec(memory_space=pltpu.SMEM)
VMEM = pl.BlockSpec(memory_space=pltpu.VMEM)


def call(kernel, outs, ins, *args, flops=0, data=0, scratch=(), mb=40):
    shapes = [jax.ShapeDtypeStruct(s, F32) for s in outs]
    return pl.pallas_call(
        kernel,
        grid=(1,),
        out_shape=shapes,
        in_specs=ins,
        out_specs=[VMEM] * len(outs),
        scratch_shapes=[pltpu.VMEM(s, F32) for s in scratch],
        compiler_params=pltpu.CompilerParams(vmem_limit_bytes=mb * 2**20),
        cost_estimate=pl.CostEstimate(flops=flops, bytes_accessed=data, transcendentals=0),
    )(*args)


def shards(tables, object_field, probe, measured, offsets, owner):
    core = lax.axis_index("core")
    piece = (2, W, W)
    top_spec = pl.BlockSpec((2, W, TILE), lambda i: (0, 0, 0))
    first, second = call(send_up_kernel, [piece, piece], [SMEM, top_spec], offsets, object_field, data=2 << 20)
    below_first = lax.ppermute(first, ALL, UP)
    below_second = lax.ppermute(second, ALL, UP)
    spread = measured.reshape(CAP, NC, CHUNK, W).transpose(1, 0, 2, 3)
    spread = lax.all_to_all(spread, COL, 0, 0, tiled=True)
    side = call(
        send_side_kernel, [piece], [SMEM, VMEM, VMEM], offsets, object_field, below_first, data=3 << 20
    )[0]
    side = lax.ppermute(side, ALL, SIDE_IN)
    picked = call(
        pick_kernel, [(NC, CHUNK, W)], [SMEM, VMEM], owner, spread.reshape(NC * CAP, CHUNK, W), data=1 << 20
    )[0]
    amp = lax.all_to_all(picked, COL, 0, 0, tiled=True).reshape(W, W)
    far, mag, patch, scale = call(
        forward_kernel,
        [(MODES, 2, W, W), (W, W), piece, (8, 128)],
        [SMEM] + [VMEM] * 5,
        offsets, object_field, below_second, side, probe, tables,
        flops=2 * 48 * W**3, data=8 << 20,
    )
    grad, give, keep = call(
        backward_kernel,
        [piece, (2, 2, W, W), (2, 2, W, W)],
        [SMEM] + [VMEM] * 6,
        offsets, far, mag, amp, patch, probe, tables,
        flops=2 * 48 * W**3, data=8 << 20, scratch=[(W, W)],
    )
    taken = lax.ppermute(give, ALL, SWAP)
    got = lax.ppermute(grad, ALL, SIDE_OUT)
    above_first = lax.ppermute(grad, ALL, DOWN)
    mine = (keep + taken).reshape(64, 16, W)
    mine = lax.all_to_all(mine, CHIPS, 0, 0, tiled=True)
    above_second = lax.ppermute(got, ALL, DOWN)
    part = jnp.sum(mine, axis=0)
    mine = lax.all_to_all(jnp.broadcast_to(part[None], (64, 16, W)), CHIPS, 0, 0, tiled=True)
    new_object = call(
        object_kernel,
        [(2, TILE, TILE)],
        [SMEM] + [VMEM] * 6,
        offsets, object_field, grad, got, above_first, above_second, scale,
        data=6 << 20,
    )[0]
    mine = mine.reshape(2, 2, W, W)
    theirs = lax.ppermute(mine, ALL, SWAP)
    total = jnp.concatenate([jnp.where(core == 0, mine, theirs), jnp.where(core == 0, theirs, mine)], axis=0)
    new_probe = probe + total / (NR * NC)
    return (new_object, new_probe)


def solution(mesh):
    inner = Mesh(mesh.devices.reshape(4, 2, 4, 4), ALL)
    tables = dft_tables()
    placed = (P(None, ("x", "core"), COL), P(), P(ALL, None, None), P(), P())

    def whole(*args):
        return shards(jnp.asarray(tables), *args)

    return jax.shard_map(
        whole, mesh=inner, in_specs=placed, out_specs=(P(None, ("x", "core"), COL), P()), check_vma=False
    )
```

```python
import functools
import math

import jax
import jax.numpy as jnp
import ml_dtypes
import numpy as np
from jax import lax
from jax.experimental import pallas as pl
from jax.experimental.pallas import tpu as pltpu
from jax.sharding import Mesh
from jax.sharding import PartitionSpec as P

W = 256
HALF = 128
TILE = 512
MODES = 4
CAP = 3
NR = 8
NC = 16
ALL = ("x", "core", "z", "y")
COL = ("z", "y")
CHIPS = ("x", "z", "y")
CHUNK = W // NC
BF = jnp.bfloat16
F32 = jnp.float32


def dft_tables():
    n = np.arange(HALF)[:, None]
    q = np.arange(HALF)[None, :]
    out = []
    for k in (2 * q, 2 * q + 1):
        angle = 2.0 * math.pi * ((n * k) % W) / W
        c = np.cos(angle) / math.sqrt(W)
        s = np.sin(angle) / math.sqrt(W)
        m = np.block([[c, -s], [s, c]])
        for t in (m, m.T):
            hi = t.astype(ml_dtypes.bfloat16)
            lo = (t - hi.astype(np.float64)).astype(ml_dtypes.bfloat16)
            out += [hi, lo]
    order = np.concatenate([np.arange(0, W, 2), np.arange(1, W, 2)])
    perm = np.zeros((W, W))
    perm[np.arange(W), order] = 1.0
    out += [perm.astype(ml_dtypes.bfloat16), perm.T.astype(ml_dtypes.bfloat16)]
    return np.stack(out)


def routes():
    up, side, slant, swap = [], [], [], []
    for r in range(NR):
        for c in range(NC):
            me = r * NC + c
            step = -1 if r % 2 == 0 else 1
            side.append((me, r * NC + (c + step) % NC))
            swap.append((me, (r ^ 1) * NC + c))
            if r > 0:
                up.append((me, me - NC))
                slant.append((me, (r - 1) * NC + (c - step) % NC))
    return up, side, slant, swap


def back(route):
    return [(b, a) for a, b in route]


UP, SIDE, SLANT, SWAP = routes()


def coords():
    core = lax.axis_index("core")
    row = lax.axis_index("x") * 2 + core
    col = lax.axis_index("z") * 4 + lax.axis_index("y")
    return row, col, core


def corner(offs, row, col):
    row = (row + NR) % NR
    col = (col + NC) % NC
    p = row * NC + col
    return offs[0, p] - row * TILE, offs[1, p] - col * TILE


def iota(shape, dim):
    return lax.broadcasted_iota(jnp.int32, shape, dim)


def fetch(pairs, sems):
    copies = []
    for n, (src, dst) in enumerate(pairs):
        copy = pltpu.make_async_copy(src, dst, sems.at[n])
        copy.start()
        copies.append(copy)
    return copies


def send_kernel(offs_hbm, tile, first, second, side, own, offs, t_buf, f_buf, s_buf, o_buf, w_buf, sems):
    row, col, core = coords()
    loads = fetch([(offs_hbm, offs), (tile.at[0], t_buf.at[0]), (tile.at[1], t_buf.at[1])], sems)
    loads[0].wait()
    even = core == 0
    _, c_up = corner(offs, row - 1, col)
    r_s, c_s = corner(offs, row, col)
    r_b, _ = corner(offs, row, col - 1)
    c1 = jnp.where(even, c_up, 0)
    c2 = jnp.where(even, 0, c_up)
    r_side, c_side = jnp.where(even, r_b, r_s), jnp.where(even, 0, c_s)
    r_own, c_own = jnp.where(even, r_s, r_b), jnp.where(even, c_s, 0)
    a = iota((W, W), 0)
    b = iota((W, W), 1)
    stores = []
    for i in range(2):
        loads[1 + i].wait()
        f_buf[i] = jnp.where(b >= c1, t_buf[i, :W, :W], t_buf[i, :W, W:])
        stores += fetch([(f_buf.at[i], first.at[i])], sems.at[pl.ds(3 + 4 * i, 1)])
        s_buf[i] = jnp.where(b >= c2, t_buf[i, :W, :W], t_buf[i, :W, W:])
        stores += fetch([(s_buf.at[i], second.at[i])], sems.at[pl.ds(4 + 4 * i, 1)])
        top = jnp.where(b >= c_side, t_buf[i, :W, :W], t_buf[i, :W, W:])
        low = jnp.where(b >= c_side, t_buf[i, W:, :W], t_buf[i, W:, W:])
        o_buf[i] = jnp.where(a >= r_side, top, low)
        stores += fetch([(o_buf.at[i], side.at[i])], sems.at[pl.ds(5 + 4 * i, 1)])
        top = jnp.where(b >= c_own, t_buf[i, :W, :W], t_buf[i, :W, W:])
        low = jnp.where(b >= c_own, t_buf[i, W:, :W], t_buf[i, W:, W:])
        w_buf[i] = jnp.where(a >= r_own, top, low)
        stores += fetch([(w_buf.at[i], own.at[i])], sems.at[pl.ds(6 + 4 * i, 1)])
    for copy in stores:
        copy.wait()


def split(x):
    hi = x.astype(BF)
    lo = (x - hi.astype(F32)).astype(BF)
    return hi, lo


def mm(a, b):
    return jnp.dot(a, b, preferred_element_type=F32)


def right(x, hi, lo):
    xh, xl = split(x)
    return mm(jnp.concatenate([xh, xh, xl], axis=1), jnp.concatenate([hi, lo, hi], axis=0))


def left(hi, lo, x):
    xh, xl = split(x)
    return mm(jnp.concatenate([hi, lo, hi], axis=1), jnp.concatenate([xh, xh, xl], axis=0))


def halves(x, axis):
    first = lax.slice_in_dim(x, 0, HALF, axis=axis)
    second = lax.slice_in_dim(x, HALF, W, axis=axis)
    return first, second


def work_kernel(
    offs_hbm, amp, own, below, side, slant, probe, tables, grad, give, keep, scale,
    offs, a_buf, o_buf, b_buf, s_buf, d_buf, p_buf, t_buf, f_buf, m_buf, x_buf, g_buf, q_buf, sems,
):
    row, col, core = coords()
    loads = fetch(
        [
            (offs_hbm, offs), (own, o_buf), (below, b_buf), (side, s_buf), (slant, d_buf),
            (tables, t_buf), (amp, a_buf),
        ],
        sems,
    )
    order = [(t + 2 * (1 - core)) % MODES for t in range(MODES)]
    p_loads = fetch([(probe.at[order[t]], p_buf.at[t]) for t in range(MODES)], sems.at[pl.ds(7, MODES)])
    loads[0].wait()
    r, c = corner(offs, row, jnp.where(core == 0, col, col - 1))
    a = iota((W, W), 0)
    b = iota((W, W), 1)
    beyond = jnp.where(c > b + W, 1, 0)
    use_side = beyond != core
    row_shift = (2 * W - r) % W
    col_shift = (2 * W - c) % W
    for n in range(1, 5):
        loads[n].wait()
    for i in range(2):
        whole = jnp.where(
            a + W >= r, jnp.where(use_side, s_buf[i], o_buf[i]), jnp.where(use_side, d_buf[i], b_buf[i])
        )
        x_buf[i] = pltpu.roll(pltpu.roll(whole, row_shift, 0), col_shift, 1)
    loads[5].wait()
    power = jnp.zeros((W, W), F32)
    for t in range(MODES):
        p_loads[t].wait()
        p_re = p_buf[t, 0]
        p_im = p_buf[t, 1]
        o_re = x_buf[0]
        o_im = x_buf[1]
        power += p_re * p_re + p_im * p_im
        e_re = p_re * o_re - p_im * o_im
        e_im = p_re * o_im + p_im * o_re
        r0, r1 = halves(e_re, 1)
        i0, i1 = halves(e_im, 1)
        even = right(jnp.concatenate([r0 + r1, i0 + i1], axis=1), t_buf[0], t_buf[1])
        odd = right(jnp.concatenate([r0 - r1, i0 - i1], axis=1), t_buf[4], t_buf[5])
        h_re = jnp.concatenate([even[:, :HALF], odd[:, :HALF]], axis=1)
        h_im = jnp.concatenate([even[:, HALF:], odd[:, HALF:]], axis=1)
        r0, r1 = halves(h_re, 0)
        i0, i1 = halves(h_im, 0)
        even = left(t_buf[2], t_buf[3], jnp.concatenate([r0 + r1, i0 + i1], axis=0))
        odd = left(t_buf[6], t_buf[7], jnp.concatenate([r0 - r1, i0 - i1], axis=0))
        f_buf[t, 0] = even
        f_buf[t, 1] = odd
        if t == 0:
            m_buf[:HALF] = even[:HALF] * even[:HALF] + even[HALF:] * even[HALF:]
            m_buf[HALF:] = odd[:HALF] * odd[:HALF] + odd[HALF:] * odd[HALF:]
        else:
            m_buf[:HALF] += even[:HALF] * even[:HALF] + even[HALF:] * even[HALF:]
            m_buf[HALF:] += odd[:HALF] * odd[:HALF] + odd[HALF:] * odd[HALF:]
    scale[...] = jnp.full(scale.shape, 1.0 / (jnp.max(power) + 1e-05), F32)
    loads[6].wait()
    x = a_buf[...]
    for turn in range(2):
        p1 = x.astype(BF)
        rest = x - p1.astype(F32)
        p2 = rest.astype(BF)
        p3 = (rest - p2.astype(F32)).astype(BF)
        if turn == 0:
            x = mm(t_buf[8], p1) + mm(t_buf[8], p2) + mm(t_buf[8], p3)
        else:
            x = mm(p1, t_buf[9]) + mm(p2, t_buf[9]) + mm(p3, t_buf[9])
    m_buf[...] = x / jnp.maximum(jnp.sqrt(m_buf[...]), 0.5) - 1.0
    stores = []
    for t in range(MODES):
        f_even = m_buf[:HALF]
        f_odd = m_buf[HALF:]
        even = f_buf[t, 0] * jnp.concatenate([f_even, f_even], axis=0)
        odd = f_buf[t, 1] * jnp.concatenate([f_odd, f_odd], axis=0)
        u = left(t_buf[0], t_buf[1], even)
        v = left(t_buf[4], t_buf[5], odd)
        h_re = jnp.concatenate([u[:HALF] + v[:HALF], u[:HALF] - v[:HALF]], axis=0)
        h_im = jnp.concatenate([u[HALF:] + v[HALF:], u[HALF:] - v[HALF:]], axis=0)
        u = right(jnp.concatenate([h_re[:, :HALF], h_im[:, :HALF]], axis=1), t_buf[2], t_buf[3])
        v = right(jnp.concatenate([h_re[:, HALF:], h_im[:, HALF:]], axis=1), t_buf[6], t_buf[7])
        b_re = jnp.concatenate([u[:, :HALF] + v[:, :HALF], u[:, :HALF] - v[:, :HALF]], axis=1)
        b_im = jnp.concatenate([u[:, HALF:] + v[:, HALF:], u[:, HALF:] - v[:, HALF:]], axis=1)
        p_re = p_buf[t, 0]
        p_im = p_buf[t, 1]
        o_re = x_buf[0]
        o_im = x_buf[1]
        g_re = p_re * b_re + p_im * b_im
        g_im = p_re * b_im - p_im * b_re
        if t == 0:
            g_buf[0] = g_re
            g_buf[1] = g_im
        else:
            g_buf[0] += g_re
            g_buf[1] += g_im
        q_buf[t, 0] = o_re * b_re + o_im * b_im
        q_buf[t, 1] = o_re * b_im - o_im * b_re
        target = give.at[t] if t < 2 else keep.at[t - 2]
        stores += fetch([(q_buf.at[t], target)], sems.at[pl.ds(11 + t, 1)])
    for i in range(2):
        g_buf[i] = pltpu.roll(pltpu.roll(g_buf[i], r % W, 0), c % W, 1)
        stores += fetch([(g_buf.at[i], grad.at[i])], sems.at[pl.ds(15 + i, 1)])
    for copy in stores:
        copy.wait()


def pick_kernel(owner_hbm, slots, out, owner, s_buf, o_buf, sems):
    row, col, core = coords()
    loads = fetch([(owner_hbm, owner), (slots, s_buf)], sems)
    loads[0].wait()
    base = row * NC
    owners = [owner[0, base + i] for i in range(NC)]
    index = []
    for i in range(NC):
        rank = jnp.int32(0)
        for q in range(i):
            rank = rank + jnp.where(owners[q] == owners[i], 1, 0)
        index.append(owners[i] * CAP + rank)
    loads[1].wait()
    for i in range(NC):
        device = jnp.where(core == 0, i, (i + 1) % NC)
        o_buf[device] = s_buf[index[i]]
    for copy in fetch([(o_buf, out)], sems.at[pl.ds(2, 1)]):
        copy.wait()


def sum_kernel(parts, out, p_buf, o_buf, sems):
    groups = 4
    per = 64 // groups
    loads = fetch(
        [(parts.at[pl.ds(g * per, per)], p_buf.at[pl.ds(g * per, per)]) for g in range(groups)], sems
    )
    total = jnp.zeros((16, W), F32)
    for g in range(groups):
        loads[g].wait()
        for n in range(per):
            total += p_buf[g * per + n]
    for n in range(8):
        o_buf[n] = total
    stores = fetch([(o_buf, out.at[pl.ds(8 * g, 8)]) for g in range(8)], sems.at[pl.ds(groups, 8)])
    for copy in stores:
        copy.wait()


def object_kernel(
    offs_hbm, scale, tile, own, got, above_first, above_second, out,
    offs, t_buf, w_buf, g_buf, f_buf, s_buf, o_buf, sems,
):
    row, col, core = coords()
    fetch([(offs_hbm, offs)], sems.at[pl.ds(12, 1)])[0].wait()
    loads = []
    for i in range(2):
        loads.append(
            fetch(
                [
                    (tile.at[i], t_buf.at[i]),
                    (own.at[i], w_buf.at[i]),
                    (got.at[i], g_buf.at[i]),
                    (above_first.at[i], f_buf.at[i]),
                    (above_second.at[i], s_buf.at[i]),
                ],
                sems.at[pl.ds(5 * i, 5)],
            )
        )
    a = iota((W, W), 0)
    b = iota((W, W), 1)
    s = scale[0, 0]
    r_s, c_s = corner(offs, row, col)
    r_b, c_b = corner(offs, row, col - 1)
    r_as, c_as = corner(offs, row - 1, col)
    r_ab, c_ab = corner(offs, row - 1, col - 1)

    def bands(at, v):
        return [v <= at, jnp.logical_and(v > at, v <= at + W)]

    even = core == 0
    rows_s, cols_s = bands(a, r_s), bands(b, c_s)
    rows_b = bands(a, r_b)
    in_b = c_b > b + W
    cols_as = bands(b, c_as)
    low_as = r_as > a + W
    low_ab = jnp.logical_and(r_ab > a + W, c_ab > b + W)
    stores = []
    for i in range(2):
        for copy in loads[i]:
            copy.wait()
        g_s = jnp.where(even, w_buf[i], g_buf[i])
        g_b = jnp.where(even, g_buf[i], w_buf[i])
        d_s = jnp.where(even, s_buf[i], f_buf[i])
        d_b = jnp.where(even, f_buf[i], s_buf[i])
        for p in range(2):
            for q in range(2):
                total = jnp.where(jnp.logical_and(rows_s[p], cols_s[q]), g_s, 0.0)
                if q == 0:
                    total += jnp.where(jnp.logical_and(rows_b[p], in_b), g_b, 0.0)
                if p == 0:
                    total += jnp.where(jnp.logical_and(low_as, cols_as[q]), d_s, 0.0)
                if p == 0 and q == 0:
                    total += jnp.where(low_ab, d_b, 0.0)
                at = (i, pl.ds(p * W, W), pl.ds(q * W, W))
                o_buf[at] = t_buf[at] + total * s
        stores += fetch([(o_buf.at[i], out.at[i])], sems.at[pl.ds(10 + i, 1)])
    for copy in stores:
        copy.wait()


def probe_kernel(probe, mine, theirs, out, p_buf, m_buf, o_buf, sems):
    core = lax.axis_index("core")
    order = [(m + 2 * core) % MODES for m in range(MODES)]
    loads = []
    for t in range(MODES):
        src = mine.at[t] if t < 2 else theirs.at[t - 2]
        loads.append(
            fetch([(probe.at[order[t]], p_buf.at[t]), (src, m_buf.at[t])], sems.at[pl.ds(2 * t, 2)])
        )
    stores = []
    for t in range(MODES):
        for copy in loads[t]:
            copy.wait()
        o_buf[t] = p_buf[t] + m_buf[t] * (1.0 / (NR * NC))
        stores += fetch([(o_buf.at[t], out.at[order[t]])], sems.at[pl.ds(8 + t, 1)])
    for copy in stores:
        copy.wait()


SMEM = pl.BlockSpec(memory_space=pltpu.SMEM)
VMEM = pl.BlockSpec(memory_space=pltpu.VMEM)
HBM = pl.BlockSpec(memory_space=pltpu.HBM)
PIECE = (2, W, W)
WORK_MB = 58


def call(kernel, outs, ins, scratch, sems, *args, flops=0, data=0, out_specs=None, mb=62):
    shapes = [jax.ShapeDtypeStruct(s, F32) for s in outs]
    buffers = [pltpu.VMEM(s, F32) if isinstance(s, tuple) else s for s in scratch]
    return pl.pallas_call(
        kernel,
        out_shape=shapes,
        in_specs=ins,
        out_specs=out_specs or [HBM] * len(outs),
        scratch_shapes=buffers + [pltpu.SemaphoreType.DMA((sems,))],
        compiler_params=pltpu.CompilerParams(vmem_limit_bytes=mb * 2**20),
        cost_estimate=pl.CostEstimate(flops=flops, bytes_accessed=data, transcendentals=0),
    )(*args)


def exchange(x):
    return lax.all_to_all(x, CHIPS, 0, 0, tiled=True)


def shards(tables, object_field, probe, measured, offsets, owner):
    offsets = offsets.T
    owner = owner.reshape(1, NR * NC)
    modes = (MODES, 2, W, W)
    half = (2, 2, W, W)
    table_buf = pltpu.VMEM(tables.shape, BF)
    offs_buf = pltpu.SMEM(offsets.shape, jnp.int32)
    owner_buf = pltpu.SMEM(owner.shape, jnp.int32)
    first, second, side, own = call(
        send_kernel, [PIECE] * 4, [HBM] * 2, [offs_buf, (2, TILE, TILE), PIECE, PIECE, PIECE, PIECE], 11,
        offsets, object_field, data=4 << 20,
    )
    side = lax.ppermute(side, ALL, SIDE)
    slant = lax.ppermute(first, ALL, SLANT)
    below = lax.ppermute(second, ALL, UP)
    spread = measured.reshape(CAP, NC, CHUNK, W).transpose(1, 0, 2, 3)
    spread = lax.all_to_all(spread, COL, 0, 0, tiled=True)
    slots = (NC * CAP, CHUNK, W)
    picked = call(
        pick_kernel, [(NC, CHUNK, W)], [HBM] * 2, [owner_buf, slots, (NC, CHUNK, W)], 3,
        owner, spread.reshape(slots), data=1 << 20, mb=50,
    )[0]
    amp = lax.all_to_all(picked, COL, 0, 0, tiled=True).reshape(W, W)
    grad, give, keep, scale = call(
        work_kernel, [PIECE, half, half, (8, 128)], [HBM] * 8,
        [offs_buf, (W, W), PIECE, PIECE, PIECE, PIECE, modes, table_buf, modes, (W, W), PIECE, PIECE, modes], 17,
        offsets, amp, own, below, side, slant, probe, tables,
        flops=2 * 96 * W**3, data=10 << 20, out_specs=[HBM, HBM, HBM, VMEM], mb=WORK_MB,
    )
    taken = lax.ppermute(give, ALL, SWAP)
    got = lax.ppermute(grad, ALL, back(SIDE))
    above_first = lax.ppermute(grad, ALL, back(UP))
    above_second = lax.ppermute(grad, ALL, back(SLANT))
    mine = (keep + taken).reshape(64, 16, W)
    inside = offsets[0, 0] >= 0
    parts = lax.cond(inside, exchange, jnp.zeros_like, mine)
    parts, got, above_first, above_second = lax.optimization_barrier((parts, got, above_first, above_second))
    copies = call(
        sum_kernel, [(64, 16, W)], [HBM], [(64, 16, W), (8, 16, W)], 12, parts, data=2 << 20, mb=50,
    )[0]
    mine = lax.all_to_all(copies, CHIPS, 0, 0, tiled=True)
    new_object = call(
        object_kernel, [(2, TILE, TILE)], [HBM, SMEM] + [HBM] * 5,
        [offs_buf, (2, TILE, TILE), PIECE, PIECE, PIECE, PIECE, (2, TILE, TILE)], 13,
        offsets, scale, object_field, grad, got, above_first, above_second, data=6 << 20,
    )[0]
    mine, new_object = lax.optimization_barrier((mine, new_object))
    mine = mine.reshape(half)
    theirs = lax.ppermute(mine, ALL, SWAP)
    new_probe = call(
        probe_kernel, [modes], [HBM] * 3, [modes, modes, modes], 12, probe, mine, theirs, data=6 << 20, mb=50,
    )[0]
    return (new_object, new_probe)


def solution(mesh):
    inner = Mesh(mesh.devices.reshape(4, 2, 4, 4), ALL)
    tables = dft_tables()
    placed = (P(None, ("x", "core"), COL), P(), P(ALL, None, None), P(), P())

    def whole(*args):
        return shards(jnp.asarray(tables), *args)

    return jax.shard_map(
        whole, mesh=inner, in_specs=placed, out_specs=(P(None, ("x", "core"), COL), P()), check_vma=False
    )
```

```python
import functools
import math

import jax
import jax.numpy as jnp
import ml_dtypes
import numpy as np
from jax import lax
from jax.experimental import pallas as pl
from jax.experimental.pallas import tpu as pltpu
from jax.sharding import Mesh
from jax.sharding import PartitionSpec as P

W = 256
HALF = 128
TILE = 512
MODES = 4
CAP = 3
NR = 8
NC = 16
ALL = ("x", "core", "z", "y")
COL = ("z", "y")
CHIPS = ("x", "z", "y")
CHUNK = W // NC
BF = jnp.bfloat16
F32 = jnp.float32


def dft_tables():
    n = np.arange(HALF)[:, None]
    q = np.arange(HALF)[None, :]
    plain, turned = [], []
    for k in (2 * q, 2 * q + 1):
        angle = 2.0 * math.pi * ((n * k) % W) / W
        c = np.cos(angle) / math.sqrt(W)
        s = np.sin(angle) / math.sqrt(W)
        m = np.block([[c, -s], [s, c]])
        for t, out in ((m, plain), (m.T, turned)):
            hi = t.astype(ml_dtypes.bfloat16)
            lo = (t - hi.astype(np.float64)).astype(ml_dtypes.bfloat16)
            out += [hi, lo]
    out = plain + turned
    order = np.concatenate([np.arange(0, W, 2), np.arange(1, W, 2)])
    perm = np.zeros((W, W))
    perm[np.arange(W), order] = 1.0
    out += [perm.astype(ml_dtypes.bfloat16), perm.T.astype(ml_dtypes.bfloat16)]
    return np.stack(out)


def routes():
    up, side, slant, swap = [], [], [], []
    for r in range(NR):
        for c in range(NC):
            me = r * NC + c
            step = -1 if r % 2 == 0 else 1
            side.append((me, r * NC + (c + step) % NC))
            swap.append((me, (r ^ 1) * NC + c))
            if r > 0:
                up.append((me, me - NC))
                slant.append((me, (r - 1) * NC + (c - step) % NC))
    return up, side, slant, swap


def back(route):
    return [(b, a) for a, b in route]


UP, SIDE, SLANT, SWAP = routes()


def coords():
    core = lax.axis_index("core")
    row = lax.axis_index("x") * 2 + core
    col = lax.axis_index("z") * 4 + lax.axis_index("y")
    return row, col, core


def corner(offs, row, col):
    row = (row + NR) % NR
    col = (col + NC) % NC
    p = row * NC + col
    return offs[0, p] - row * TILE, offs[1, p] - col * TILE


def iota(shape, dim):
    return lax.broadcasted_iota(jnp.int32, shape, dim)


def fetch(pairs, sems):
    copies = []
    for n, (src, dst) in enumerate(pairs):
        copy = pltpu.make_async_copy(src, dst, sems.at[n])
        copy.start()
        copies.append(copy)
    return copies


def send_up_kernel(offs_hbm, tile, first, second, offs, t_buf, f_buf, s_buf, sems):
    row, col, core = coords()
    loads = fetch([(offs_hbm, offs)] + [(tile.at[i, pl.ds(0, W)], t_buf.at[i]) for i in range(2)], sems)
    loads[0].wait()
    _, c = corner(offs, row - 1, col)
    b = iota((W, W), 1)
    c1 = jnp.where(core == 1, 0, c)
    c2 = jnp.where(core == 1, c, 0)
    stores = []
    for i in range(2):
        loads[1 + i].wait()
        f_buf[i] = jnp.where(b >= c1, t_buf[i, :, :W], t_buf[i, :, W:])
        stores += fetch([(f_buf.at[i], first.at[i])], sems.at[pl.ds(3 + 2 * i, 1)])
        s_buf[i] = jnp.where(b >= c2, t_buf[i, :, :W], t_buf[i, :, W:])
        stores += fetch([(s_buf.at[i], second.at[i])], sems.at[pl.ds(4 + 2 * i, 1)])
    for copy in stores:
        copy.wait()


def send_side_kernel(offs_hbm, tile, below, side, own, offs, t_buf, b_buf, o_buf, w_buf, sems):
    row, col, core = coords()
    loads = fetch([(offs_hbm, offs)], sems)
    for i in range(2):
        loads += fetch([(tile.at[i], t_buf.at[i]), (below.at[i], b_buf.at[i])], sems.at[pl.ds(1 + 2 * i, 2)])
    loads[0].wait()
    even = core == 0
    r_s, c_s = corner(offs, row, col)
    r_b, _ = corner(offs, row, col - 1)
    r_side, c_side = jnp.where(even, r_b, r_s), jnp.where(even, 0, c_s)
    r_own, c_own = jnp.where(even, r_s, r_b), jnp.where(even, c_s, 0)
    a = iota((W, W), 0)
    b = iota((W, W), 1)
    stores = []
    for i in range(2):
        loads[1 + 2 * i].wait()
        loads[2 + 2 * i].wait()
        top = jnp.where(b >= c_side, t_buf[i, :W, :W], t_buf[i, :W, W:])
        low = jnp.where(b >= c_side, t_buf[i, W:, :W], t_buf[i, W:, W:])
        o_buf[i] = jnp.where(a >= r_side, top, jnp.where(a + W >= r_side, low, b_buf[i]))
        stores += fetch([(o_buf.at[i], side.at[i])], sems.at[pl.ds(5 + 2 * i, 1)])
        top = jnp.where(b >= c_own, t_buf[i, :W, :W], t_buf[i, :W, W:])
        low = jnp.where(b >= c_own, t_buf[i, W:, :W], t_buf[i, W:, W:])
        w_buf[i] = jnp.where(a >= r_own, top, low)
        stores += fetch([(w_buf.at[i], own.at[i])], sems.at[pl.ds(6 + 2 * i, 1)])
    for copy in stores:
        copy.wait()


def split(x):
    hi = x.astype(BF)
    lo = (x - hi.astype(F32)).astype(BF)
    return hi, lo


def mm(a, b):
    return jnp.dot(a, b, preferred_element_type=F32)


STRIP = 32


def strips(rows):
    return range(0, rows, STRIP)


def put_split(ref, at, x):
    hi, lo = split(x)
    ref[0, pl.ds(at, STRIP)] = hi
    ref[1, pl.ds(at, STRIP)] = lo


def right(x, hi, lo):
    return mm(jnp.concatenate([x[0], x[0], x[1]], axis=1), jnp.concatenate([hi, lo, hi], axis=0))


def left(hi, lo, x):
    return mm(jnp.concatenate([hi, lo, hi], axis=1), jnp.concatenate([x[0], x[0], x[1]], axis=0))


def lanes(a, b):
    return jnp.concatenate([a, b], axis=1)


def forward_kernel(
    offs_hbm, own, below, side, probe, tables, far, mag, patch, scale,
    offs, o_buf, b_buf, s_buf, p_buf, t_buf, f_buf, m_buf, x_buf, g_buf, rows_in, cols_in, h_buf, sems,
):
    row, col, core = coords()
    loads = fetch([(offs_hbm, offs), (own, o_buf), (below, b_buf), (side, s_buf)], sems)
    p_loads = fetch([(probe.at[0], p_buf.at[0])], sems.at[pl.ds(4, 1)])
    loads += fetch([(tables.at[pl.ds(0, 4)], t_buf.at[pl.ds(0, 4)])], sems.at[pl.ds(5, 1)])
    loads[0].wait()
    r, c = corner(offs, row, jnp.where(core == 0, col, col - 1))
    a = iota((W, W), 0)
    b = iota((W, W), 1)
    beyond = jnp.where(c > b + W, 1, 0)
    use_side = beyond != core
    row_shift = (2 * W - r) % W
    col_shift = (2 * W - c) % W
    for n in range(1, 4):
        loads[n].wait()
    loads += fetch([(tables.at[pl.ds(4, 4)], t_buf.at[pl.ds(4, 4)])], sems.at[pl.ds(15, 1)])
    p_loads += fetch([(probe.at[m], p_buf.at[m]) for m in range(1, MODES)], sems.at[pl.ds(6, MODES - 1)])
    for i in range(2):
        whole = jnp.where(use_side, s_buf[i], jnp.where(a + W >= r, o_buf[i], b_buf[i]))
        x_buf[i] = pltpu.roll(pltpu.roll(whole, row_shift, 0), col_shift, 1)

    stores = fetch([(x_buf, patch)], sems.at[pl.ds(9, 1)])

    def enter(t):
        p_loads[t].wait()
        for k in strips(W):
            at = pl.ds(k, STRIP)
            p_re, p_im = p_buf[t, 0, at], p_buf[t, 1, at]
            o_re, o_im = x_buf[0, at], x_buf[1, at]
            e_re = p_re * o_re - p_im * o_im
            e_im = p_re * o_im + p_im * o_re
            power = p_re * p_re + p_im * p_im
            g_buf[at] = power if t == 0 else g_buf[at] + power
            r0, r1 = e_re[:, :HALF], e_re[:, HALF:]
            i0, i1 = e_im[:, :HALF], e_im[:, HALF:]
            put_split(rows_in.at[t, 0], k, lanes(r0 + r1, i0 + i1))
            put_split(rows_in.at[t, 1], k, lanes(r0 - r1, i0 - i1))

    def along_rows(t):
        h_buf[t, 0] = right(rows_in[t, 0], t_buf[0], t_buf[1])
        h_buf[t, 1] = right(rows_in[t, 1], t_buf[2], t_buf[3])
        for k in strips(HALF):
            near, away = pl.ds(k, STRIP), pl.ds(HALF + k, STRIP)
            e0, e1 = h_buf[t, 0, near], h_buf[t, 0, away]
            o0, o1 = h_buf[t, 1, near], h_buf[t, 1, away]
            e_sum, e_dif, o_sum, o_dif = e0 + e1, e0 - e1, o0 + o1, o0 - o1
            put_split(cols_in.at[t, 0], k, lanes(e_sum[:, :HALF], o_sum[:, :HALF]))
            put_split(cols_in.at[t, 0], HALF + k, lanes(e_sum[:, HALF:], o_sum[:, HALF:]))
            put_split(cols_in.at[t, 1], k, lanes(e_dif[:, :HALF], o_dif[:, :HALF]))
            put_split(cols_in.at[t, 1], HALF + k, lanes(e_dif[:, HALF:], o_dif[:, HALF:]))

    def along_cols(t):
        f_buf[t, 0] = left(t_buf[4], t_buf[5], cols_in[t, 0])
        f_buf[t, 1] = left(t_buf[6], t_buf[7], cols_in[t, 1])
        stores.extend(fetch([(f_buf.at[t], far.at[t])], sems.at[pl.ds(10 + t, 1)]))
        for k in strips(HALF):
            near, away = pl.ds(k, STRIP), pl.ds(HALF + k, STRIP)
            for p, at in ((0, near), (1, away)):
                x, y = f_buf[t, p, near], f_buf[t, p, away]
                z = x * x + y * y
                m_buf[at] = z if t == 0 else m_buf[at] + z

    enter(0)
    loads[4].wait()
    loads[5].wait()
    for t in range(MODES):
        along_rows(t)
        if t + 1 < MODES:
            enter(t + 1)
        along_cols(t)
    for k in strips(W):
        at = pl.ds(k, STRIP)
        m_buf[at] = jnp.maximum(jnp.sqrt(m_buf[at]), 0.5)
    stores += fetch([(m_buf, mag)], sems.at[pl.ds(14, 1)])
    scale[...] = jnp.full(scale.shape, 1.0 / (jnp.max(g_buf[...]) + 1e-05), F32)
    for copy in stores:
        copy.wait()


def backward_kernel(
    offs_hbm, amp, far, mag, patch, probe, tables, grad, give, keep,
    offs, a_buf, m_buf, t_buf, f_buf, x_buf, p_buf, g_buf, q_buf, rows_in, cols_in, h_buf, sems,
):
    row, col, core = coords()
    order = [(t + 2 * (1 - core)) % MODES for t in range(MODES)]
    loads = fetch([(amp, a_buf), (tables.at[pl.ds(8, 2)], t_buf.at[pl.ds(8, 2)]), (mag, m_buf)], sems)
    t_loads = fetch([(tables.at[pl.ds(0, 4)], t_buf.at[pl.ds(0, 4)])], sems.at[pl.ds(19, 1)])
    f_loads = fetch([(far.at[order[0]], f_buf.at[0])], sems.at[pl.ds(3, 1)])
    loads[0].wait()
    loads[1].wait()
    x = a_buf[...]
    for turn in range(2):
        p1 = x.astype(BF)
        rest = x - p1.astype(F32)
        p2 = rest.astype(BF)
        p3 = (rest - p2.astype(F32)).astype(BF)
        if turn == 0:
            x = mm(t_buf[8], p1) + mm(t_buf[8], p2) + mm(t_buf[8], p3)
        else:
            x = mm(p1, t_buf[9]) + mm(p2, t_buf[9]) + mm(p3, t_buf[9])
    a_buf[...] = x
    loads[2].wait()
    f_loads[0].wait()
    t_loads += fetch([(tables.at[pl.ds(4, 4)], t_buf.at[pl.ds(4, 4)])], sems.at[pl.ds(20, 1)])
    loads += fetch([(patch, x_buf), (probe.at[order[0]], p_buf.at[0])], sems.at[pl.ds(4, 2)])
    f_loads += fetch([(far.at[order[t]], f_buf.at[t]) for t in range(1, MODES)], sems.at[pl.ds(6, MODES - 1)])
    p_loads = fetch([(probe.at[order[t]], p_buf.at[t]) for t in range(1, MODES)], sems.at[pl.ds(9, MODES - 1)])
    loads += fetch([(offs_hbm, offs)], sems.at[pl.ds(12, 1)])
    for k in strips(W):
        at = pl.ds(k, STRIP)
        m_buf[at] = a_buf[at] / m_buf[at] - 1.0

    def weigh(t):
        for k in strips(HALF):
            near, away = pl.ds(k, STRIP), pl.ds(HALF + k, STRIP)
            for p, at in ((0, near), (1, away)):
                put_split(cols_in.at[t, p], k, f_buf[t, p, near] * m_buf[at])
                put_split(cols_in.at[t, p], HALF + k, f_buf[t, p, away] * m_buf[at])

    def back_cols(t):
        h_buf[t, 0] = left(t_buf[0], t_buf[1], cols_in[t, 0])
        h_buf[t, 1] = left(t_buf[2], t_buf[3], cols_in[t, 1])
        for k in strips(HALF):
            near, away = pl.ds(k, STRIP), pl.ds(HALF + k, STRIP)
            u_re, v_re = h_buf[t, 0, near], h_buf[t, 1, near]
            u_im, v_im = h_buf[t, 0, away], h_buf[t, 1, away]
            for at, re, im in ((k, u_re + v_re, u_im + v_im), (HALF + k, u_re - v_re, u_im - v_im)):
                put_split(rows_in.at[t, 0], at, lanes(re[:, :HALF], im[:, :HALF]))
                put_split(rows_in.at[t, 1], at, lanes(re[:, HALF:], im[:, HALF:]))

    stores = []

    def back_rows(t):
        h_buf[t, 0] = right(rows_in[t, 0], t_buf[4], t_buf[5])
        h_buf[t, 1] = right(rows_in[t, 1], t_buf[6], t_buf[7])
        for k in strips(W):
            at = pl.ds(k, STRIP)
            u, v = h_buf[t, 0, at], h_buf[t, 1, at]
            add, sub = u + v, u - v
            b_re = lanes(add[:, :HALF], sub[:, :HALF])
            b_im = lanes(add[:, HALF:], sub[:, HALF:])
            p_re, p_im = p_buf[t, 0, at], p_buf[t, 1, at]
            o_re, o_im = x_buf[0, at], x_buf[1, at]
            g_re = p_re * b_re + p_im * b_im
            g_im = p_re * b_im - p_im * b_re
            g_buf[0, at] = g_re if t == 0 else g_buf[0, at] + g_re
            g_buf[1, at] = g_im if t == 0 else g_buf[1, at] + g_im
            q_buf[t, 0, at] = o_re * b_re + o_im * b_im
            q_buf[t, 1, at] = o_re * b_im - o_im * b_re
        target = give.at[t] if t < 2 else keep.at[t - 2]
        stores.extend(fetch([(q_buf.at[t], target)], sems.at[pl.ds(13 + t, 1)]))

    weigh(0)
    t_loads[0].wait()
    for t in range(MODES):
        back_cols(t)
        if t == 0:
            t_loads[1].wait()
            loads[3].wait()
            loads[4].wait()
        if t + 1 < MODES:
            f_loads[t + 1].wait()
            weigh(t + 1)
            p_loads[t].wait()
        back_rows(t)
    loads[5].wait()
    r, c = corner(offs, row, jnp.where(core == 0, col, col - 1))
    for i in range(2):
        g_buf[i] = pltpu.roll(pltpu.roll(g_buf[i], r % W, 0), c % W, 1)
        stores += fetch([(g_buf.at[i], grad.at[i])], sems.at[pl.ds(17 + i, 1)])
    for copy in stores:
        copy.wait()


def pick_kernel(owner_hbm, slots, out, owner, s_buf, o_buf, sems):
    row, col, core = coords()
    loads = fetch([(owner_hbm, owner), (slots, s_buf)], sems)
    loads[0].wait()
    base = row * NC
    owners = [owner[0, base + i] for i in range(NC)]
    index = []
    for i in range(NC):
        rank = jnp.int32(0)
        for q in range(i):
            rank = rank + jnp.where(owners[q] == owners[i], 1, 0)
        index.append(owners[i] * CAP + rank)
    loads[1].wait()
    for i in range(NC):
        device = jnp.where(core == 0, i, (i + 1) % NC)
        o_buf[device] = s_buf[index[i]]
    for copy in fetch([(o_buf, out)], sems.at[pl.ds(2, 1)]):
        copy.wait()


def sum_kernel(parts, out, p_buf, o_buf, sems):
    groups = 4
    per = 64 // groups
    loads = fetch(
        [(parts.at[pl.ds(g * per, per)], p_buf.at[pl.ds(g * per, per)]) for g in range(groups)], sems
    )
    total = jnp.zeros((16, W), F32)
    for g in range(groups):
        loads[g].wait()
        for n in range(per):
            total += p_buf[g * per + n]
    for n in range(8):
        o_buf[n] = total
    stores = fetch([(o_buf, out.at[pl.ds(8 * g, 8)]) for g in range(8)], sems.at[pl.ds(groups, 8)])
    for copy in stores:
        copy.wait()


def object_kernel(
    offs_hbm, scale, tile, own, got, above_first, above_second, out,
    offs, t_buf, w_buf, g_buf, f_buf, s_buf, o_buf, sems,
):
    row, col, core = coords()
    fetch([(offs_hbm, offs)], sems.at[pl.ds(12, 1)])[0].wait()
    loads = []
    for i in range(2):
        loads.append(
            fetch(
                [
                    (tile.at[i], t_buf.at[i]),
                    (own.at[i], w_buf.at[i]),
                    (got.at[i], g_buf.at[i]),
                    (above_first.at[i], f_buf.at[i]),
                    (above_second.at[i], s_buf.at[i]),
                ],
                sems.at[pl.ds(5 * i, 5)],
            )
        )
    a = iota((W, W), 0)
    b = iota((W, W), 1)
    s = scale[0, 0]
    r_s, c_s = corner(offs, row, col)
    r_b, c_b = corner(offs, row, col - 1)
    r_as, c_as = corner(offs, row - 1, col)
    r_ab, c_ab = corner(offs, row - 1, col - 1)

    def bands(at, v):
        return [v <= at, jnp.logical_and(v > at, v <= at + W)]

    even = core == 0
    rows_s, cols_s = bands(a, r_s), bands(b, c_s)
    rows_b = bands(a, r_b)
    in_b = c_b > b + W
    cols_as = bands(b, c_as)
    low_as = r_as > a + W
    low_ab = jnp.logical_and(r_ab > a + W, c_ab > b + W)
    stores = []
    for i in range(2):
        for copy in loads[i]:
            copy.wait()
        g_s = jnp.where(even, w_buf[i], g_buf[i])
        g_b = jnp.where(even, g_buf[i], w_buf[i])
        d_s = jnp.where(even, s_buf[i], f_buf[i])
        d_b = jnp.where(even, f_buf[i], s_buf[i])
        for p in range(2):
            for q in range(2):
                total = jnp.where(jnp.logical_and(rows_s[p], cols_s[q]), g_s, 0.0)
                if q == 0:
                    total += jnp.where(jnp.logical_and(rows_b[p], in_b), g_b, 0.0)
                if p == 0:
                    total += jnp.where(jnp.logical_and(low_as, cols_as[q]), d_s, 0.0)
                if p == 0 and q == 0:
                    total += jnp.where(low_ab, d_b, 0.0)
                at = (i, pl.ds(p * W, W), pl.ds(q * W, W))
                o_buf[at] = t_buf[at] + total * s
        stores += fetch([(o_buf.at[i], out.at[i])], sems.at[pl.ds(10 + i, 1)])
    for copy in stores:
        copy.wait()


def probe_kernel(first, probe, total, *refs):
    out, p_buf, m_buf, o_buf, sems = refs[-5:]
    core = lax.axis_index("core")
    base = 2 * jnp.where(first, core, 1 - core)
    loads = []
    for t in range(2):
        loads.append(
            fetch([(probe.at[base + t], p_buf.at[t]), (total.at[t], m_buf.at[t])], sems.at[pl.ds(2 * t, 2)])
        )
    stores = []
    for t in range(2):
        for copy in loads[t]:
            copy.wait()
        o_buf[t] = p_buf[t] + m_buf[t] * (1.0 / (NR * NC))
        stores += fetch([(o_buf.at[t], out.at[base + t])], sems.at[pl.ds(4 + t, 1)])
    for copy in stores:
        copy.wait()


SMEM = pl.BlockSpec(memory_space=pltpu.SMEM)
VMEM = pl.BlockSpec(memory_space=pltpu.VMEM)
HBM = pl.BlockSpec(memory_space=pltpu.HBM)
PIECE = (2, W, W)
WORK_MB = 60


def call(kernel, outs, ins, scratch, sems, *args, flops=0, data=0, out_specs=None, mb=62, alias=()):
    shapes = [jax.ShapeDtypeStruct(s, F32) for s in outs]
    buffers = [pltpu.VMEM(s, F32) if isinstance(s, tuple) else s for s in scratch]
    return pl.pallas_call(
        kernel,
        out_shape=shapes,
        in_specs=ins,
        out_specs=out_specs or [HBM] * len(outs),
        input_output_aliases=dict(alias),
        scratch_shapes=buffers + [pltpu.SemaphoreType.DMA((sems,))],
        compiler_params=pltpu.CompilerParams(vmem_limit_bytes=mb * 2**20),
        cost_estimate=pl.CostEstimate(flops=flops, bytes_accessed=data, transcendentals=0),
    )(*args)


def exchange(x):
    return lax.all_to_all(x, CHIPS, 0, 0, tiled=True)


def shards(tables, object_field, probe, measured, offsets, owner):
    offsets = offsets.T
    owner = owner.reshape(1, NR * NC)
    modes = (MODES, 2, W, W)
    half = (2, 2, W, W)
    split_buf = pltpu.VMEM((MODES, 2, 2, W, W), BF)
    table_buf = pltpu.VMEM(tables.shape, BF)
    offs_buf = pltpu.SMEM(offsets.shape, jnp.int32)
    owner_buf = pltpu.SMEM(owner.shape, jnp.int32)
    first, second = call(
        send_up_kernel, [PIECE] * 2, [HBM] * 2, [offs_buf, (2, W, TILE), PIECE, PIECE], 7,
        offsets, object_field, data=3 << 20,
    )
    below_first = lax.ppermute(first, ALL, UP)
    below = lax.ppermute(second, ALL, UP)
    side, own = call(
        send_side_kernel, [PIECE] * 2, [HBM] * 3, [offs_buf, (2, TILE, TILE), PIECE, PIECE, PIECE], 9,
        offsets, object_field, below_first, data=4 << 20,
    )
    side = lax.ppermute(side, ALL, SIDE)
    spread = measured.reshape(CAP, NC, CHUNK, W).transpose(1, 0, 2, 3)
    spread = lax.all_to_all(spread, COL, 0, 0, tiled=True)
    slots = (NC * CAP, CHUNK, W)
    picked = call(
        pick_kernel, [(NC, CHUNK, W)], [HBM] * 2, [owner_buf, slots, (NC, CHUNK, W)], 3,
        owner, spread.reshape(slots), data=1 << 20, mb=50,
    )[0]
    amp = lax.all_to_all(picked, COL, 0, 0, tiled=True).reshape(W, W)
    far, mag, patch, scale = call(
        forward_kernel, [modes, (W, W), PIECE, (8, 128)], [HBM] * 6,
        [offs_buf, PIECE, PIECE, PIECE, modes, pltpu.VMEM((8, W, W), BF), modes, (W, W), PIECE, (W, W),
         split_buf, split_buf, modes], 16,
        offsets, own, below, side, probe, tables,
        flops=2 * 48 * W**3, data=8 << 20, out_specs=[HBM, HBM, HBM, VMEM], mb=WORK_MB,
    )
    grad, give, keep = call(
        backward_kernel, [PIECE, half, half], [HBM] * 7,
        [offs_buf, (W, W), (W, W), table_buf, modes, PIECE, modes, PIECE, modes,
         split_buf, split_buf, modes], 21,
        offsets, amp, far, mag, patch, probe, tables,
        flops=2 * 48 * W**3, data=8 << 20, mb=WORK_MB,
    )
    taken = lax.ppermute(give, ALL, SWAP)
    got = lax.ppermute(grad, ALL, back(SIDE))
    above_first = lax.ppermute(grad, ALL, back(UP))
    above_second = lax.ppermute(grad, ALL, back(SLANT))
    mine = (keep + taken).reshape(64, 16, W)
    inside = offsets[0, 0] >= 0
    parts = lax.cond(inside, exchange, jnp.zeros_like, mine)
    parts, got, above_first, above_second = lax.optimization_barrier((parts, got, above_first, above_second))
    copies = call(
        sum_kernel, [(64, 16, W)], [HBM], [(64, 16, W), (8, 16, W)], 12, parts, data=2 << 20, mb=50,
    )[0]
    mine = lax.all_to_all(copies, CHIPS, 0, 0, tiled=True)
    new_object = call(
        object_kernel, [(2, TILE, TILE)], [HBM, SMEM] + [HBM] * 5,
        [offs_buf, (2, TILE, TILE), PIECE, PIECE, PIECE, PIECE, (2, TILE, TILE)], 13,
        offsets, scale, object_field, grad, got, above_first, above_second, data=6 << 20,
    )[0]
    mine, new_object = lax.optimization_barrier((mine, new_object))
    mine = mine.reshape(half)
    theirs = lax.ppermute(mine, ALL, SWAP)
    new_probe = call(
        functools.partial(probe_kernel, True), [modes], [HBM] * 2, [half, half, half], 6,
        probe, mine, data=3 << 20, mb=50,
    )[0]
    new_probe = call(
        functools.partial(probe_kernel, False), [modes], [HBM] * 3, [half, half, half], 6,
        probe, theirs, new_probe, data=3 << 20, mb=50, alias=((2, 0),),
    )[0]
    return (new_object, new_probe)


def solution(mesh):
    inner = Mesh(mesh.devices.reshape(4, 2, 4, 4), ALL)
    tables = dft_tables()
    placed = (P(None, ("x", "core"), COL), P(), P(ALL, None, None), P(), P())

    def whole(*args):
        return shards(jnp.asarray(tables), *args)

    return jax.shard_map(
        whole, mesh=inner, in_specs=placed, out_specs=(P(None, ("x", "core"), COL), P()), check_vma=False
    )
```

```python
import functools
import math

import jax
import jax.numpy as jnp
import ml_dtypes
import numpy as np
from jax import lax
from jax.experimental import pallas as pl
from jax.experimental.pallas import tpu as pltpu
from jax.sharding import Mesh
from jax.sharding import PartitionSpec as P

W = 256
HALF = 128
TILE = 512
MODES = 4
CAP = 3
NR = 8
NC = 16
ALL = ("x", "core", "z", "y")
COL = ("z", "y")
CHIPS = ("x", "z", "y")
CHUNK = W // NC
BF = jnp.bfloat16
F32 = jnp.float32


def dft_tables():
    n = np.arange(HALF)[:, None]
    q = np.arange(HALF)[None, :]
    plain, turned = [], []
    for k in (2 * q, 2 * q + 1):
        angle = 2.0 * math.pi * ((n * k) % W) / W
        c = np.cos(angle) / math.sqrt(W)
        s = np.sin(angle) / math.sqrt(W)
        m = np.block([[c, -s], [s, c]])
        for t, out in ((m, plain), (m.T, turned)):
            hi = t.astype(ml_dtypes.bfloat16)
            lo = (t - hi.astype(np.float64)).astype(ml_dtypes.bfloat16)
            out += [hi, lo]
    out = plain + turned
    order = np.concatenate([np.arange(0, W, 2), np.arange(1, W, 2)])
    perm = np.zeros((W, W))
    perm[np.arange(W), order] = 1.0
    out += [perm.astype(ml_dtypes.bfloat16), perm.T.astype(ml_dtypes.bfloat16)]
    return np.stack(out)


def routes():
    up, side, slant, swap = [], [], [], []
    for r in range(NR):
        for c in range(NC):
            me = r * NC + c
            step = -1 if r % 2 == 0 else 1
            side.append((me, r * NC + (c + step) % NC))
            swap.append((me, (r ^ 1) * NC + c))
            if r > 0:
                up.append((me, me - NC))
                slant.append((me, (r - 1) * NC + (c - step) % NC))
    return up, side, slant, swap


def back(route):
    return [(b, a) for a, b in route]


UP, SIDE, SLANT, SWAP = routes()


def coords():
    core = lax.axis_index("core")
    row = lax.axis_index("x") * 2 + core
    col = lax.axis_index("z") * 4 + lax.axis_index("y")
    return row, col, core


def corner(offs, row, col):
    row = (row + NR) % NR
    col = (col + NC) % NC
    p = row * NC + col
    return offs[0, p] - row * TILE, offs[1, p] - col * TILE


def iota(shape, dim):
    return lax.broadcasted_iota(jnp.int32, shape, dim)


def fetch(pairs, sems):
    copies = []
    for n, (src, dst) in enumerate(pairs):
        copy = pltpu.make_async_copy(src, dst, sems.at[n])
        copy.start()
        copies.append(copy)
    return copies


def send_up_kernel(offs_hbm, tile, first, second, offs, t_buf, f_buf, s_buf, sems):
    row, col, core = coords()
    loads = fetch([(offs_hbm, offs)] + [(tile.at[i, pl.ds(0, W)], t_buf.at[i]) for i in range(2)], sems)
    loads[0].wait()
    _, c = corner(offs, row - 1, col)
    b = iota((W, W), 1)
    c1 = jnp.where(core == 1, 0, c)
    c2 = jnp.where(core == 1, c, 0)
    stores = []
    for i in range(2):
        loads[1 + i].wait()
        f_buf[i] = jnp.where(b >= c1, t_buf[i, :, :W], t_buf[i, :, W:])
        stores += fetch([(f_buf.at[i], first.at[i])], sems.at[pl.ds(3 + 2 * i, 1)])
        s_buf[i] = jnp.where(b >= c2, t_buf[i, :, :W], t_buf[i, :, W:])
        stores += fetch([(s_buf.at[i], second.at[i])], sems.at[pl.ds(4 + 2 * i, 1)])
    for copy in stores:
        copy.wait()


def send_side_kernel(offs_hbm, tile, below, side, own, offs, t_buf, b_buf, o_buf, w_buf, sems):
    row, col, core = coords()
    loads = fetch([(offs_hbm, offs)], sems)
    for i in range(2):
        loads += fetch([(tile.at[i], t_buf.at[i]), (below.at[i], b_buf.at[i])], sems.at[pl.ds(1 + 2 * i, 2)])
    loads[0].wait()
    even = core == 0
    r_s, c_s = corner(offs, row, col)
    r_b, _ = corner(offs, row, col - 1)
    r_side, c_side = jnp.where(even, r_b, r_s), jnp.where(even, 0, c_s)
    r_own, c_own = jnp.where(even, r_s, r_b), jnp.where(even, c_s, 0)
    a = iota((W, W), 0)
    b = iota((W, W), 1)
    stores = []
    for i in range(2):
        loads[1 + 2 * i].wait()
        loads[2 + 2 * i].wait()
        top = jnp.where(b >= c_side, t_buf[i, :W, :W], t_buf[i, :W, W:])
        low = jnp.where(b >= c_side, t_buf[i, W:, :W], t_buf[i, W:, W:])
        o_buf[i] = jnp.where(a >= r_side, top, jnp.where(a + W >= r_side, low, b_buf[i]))
        stores += fetch([(o_buf.at[i], side.at[i])], sems.at[pl.ds(5 + 2 * i, 1)])
        top = jnp.where(b >= c_own, t_buf[i, :W, :W], t_buf[i, :W, W:])
        low = jnp.where(b >= c_own, t_buf[i, W:, :W], t_buf[i, W:, W:])
        w_buf[i] = jnp.where(a >= r_own, top, low)
        stores += fetch([(w_buf.at[i], own.at[i])], sems.at[pl.ds(6 + 2 * i, 1)])
    for copy in stores:
        copy.wait()


def split(x):
    hi = x.astype(BF)
    lo = (x - hi.astype(F32)).astype(BF)
    return hi, lo


def mm(a, b):
    return jnp.dot(a, b, preferred_element_type=F32)


STRIP = 32


def strips(rows):
    return range(0, rows, STRIP)


def put_split(ref, at, x):
    hi, lo = split(x)
    ref[0, pl.ds(at, STRIP)] = hi
    ref[1, pl.ds(at, STRIP)] = lo


def right(x, hi, lo):
    return mm(jnp.concatenate([x[0], x[0], x[1]], axis=1), jnp.concatenate([hi, lo, hi], axis=0))


def left(hi, lo, x):
    return mm(jnp.concatenate([hi, lo, hi], axis=1), jnp.concatenate([x[0], x[0], x[1]], axis=0))


def lanes(a, b):
    return jnp.concatenate([a, b], axis=1)


def forward_kernel(
    offs_hbm, own, below, side, probe, tables, far, mag, patch, scale,
    offs, o_buf, b_buf, s_buf, p_buf, t_buf, f_buf, m_buf, x_buf, g_buf, rows_in, cols_in, h_buf, sems,
):
    row, col, core = coords()
    loads = fetch([(offs_hbm, offs), (own, o_buf), (below, b_buf), (side, s_buf)], sems)
    p_loads = fetch([(probe.at[0], p_buf.at[0])], sems.at[pl.ds(4, 1)])
    loads += fetch([(tables.at[pl.ds(0, 4)], t_buf.at[pl.ds(0, 4)])], sems.at[pl.ds(5, 1)])
    loads[0].wait()
    r, c = corner(offs, row, jnp.where(core == 0, col, col - 1))
    a = iota((W, W), 0)
    b = iota((W, W), 1)
    beyond = jnp.where(c > b + W, 1, 0)
    use_side = beyond != core
    row_shift = (2 * W - r) % W
    col_shift = (2 * W - c) % W
    for n in range(1, 4):
        loads[n].wait()
    loads += fetch([(tables.at[pl.ds(4, 4)], t_buf.at[pl.ds(4, 4)])], sems.at[pl.ds(15, 1)])
    p_loads += fetch([(probe.at[m], p_buf.at[m]) for m in range(1, MODES)], sems.at[pl.ds(6, MODES - 1)])
    for i in range(2):
        whole = jnp.where(use_side, s_buf[i], jnp.where(a + W >= r, o_buf[i], b_buf[i]))
        x_buf[i] = pltpu.roll(pltpu.roll(whole, row_shift, 0), col_shift, 1)

    stores = fetch([(x_buf, patch)], sems.at[pl.ds(9, 1)])

    def enter(t):
        p_loads[t].wait()
        for k in strips(W):
            at = pl.ds(k, STRIP)
            p_re, p_im = p_buf[t, 0, at], p_buf[t, 1, at]
            o_re, o_im = x_buf[0, at], x_buf[1, at]
            e_re = p_re * o_re - p_im * o_im
            e_im = p_re * o_im + p_im * o_re
            power = p_re * p_re + p_im * p_im
            g_buf[at] = power if t == 0 else g_buf[at] + power
            r0, r1 = e_re[:, :HALF], e_re[:, HALF:]
            i0, i1 = e_im[:, :HALF], e_im[:, HALF:]
            put_split(rows_in.at[t, 0], k, lanes(r0 + r1, i0 + i1))
            put_split(rows_in.at[t, 1], k, lanes(r0 - r1, i0 - i1))

    def along_rows(t):
        h_buf[t, 0] = right(rows_in[t, 0], t_buf[0], t_buf[1])
        h_buf[t, 1] = right(rows_in[t, 1], t_buf[2], t_buf[3])
        for k in strips(HALF):
            near, away = pl.ds(k, STRIP), pl.ds(HALF + k, STRIP)
            e0, e1 = h_buf[t, 0, near], h_buf[t, 0, away]
            o0, o1 = h_buf[t, 1, near], h_buf[t, 1, away]
            e_sum, e_dif, o_sum, o_dif = e0 + e1, e0 - e1, o0 + o1, o0 - o1
            put_split(cols_in.at[t, 0], k, lanes(e_sum[:, :HALF], o_sum[:, :HALF]))
            put_split(cols_in.at[t, 0], HALF + k, lanes(e_sum[:, HALF:], o_sum[:, HALF:]))
            put_split(cols_in.at[t, 1], k, lanes(e_dif[:, :HALF], o_dif[:, :HALF]))
            put_split(cols_in.at[t, 1], HALF + k, lanes(e_dif[:, HALF:], o_dif[:, HALF:]))

    def along_cols(t):
        f_buf[t, 0] = left(t_buf[4], t_buf[5], cols_in[t, 0])
        f_buf[t, 1] = left(t_buf[6], t_buf[7], cols_in[t, 1])
        stores.extend(fetch([(f_buf.at[t], far.at[t])], sems.at[pl.ds(10 + t, 1)]))
        for k in strips(HALF):
            near, away = pl.ds(k, STRIP), pl.ds(HALF + k, STRIP)
            for p, at in ((0, near), (1, away)):
                x, y = f_buf[t, p, near], f_buf[t, p, away]
                z = x * x + y * y
                m_buf[at] = z if t == 0 else m_buf[at] + z

    enter(0)
    loads[4].wait()
    loads[5].wait()
    for t in range(MODES):
        along_rows(t)
        if t + 1 < MODES:
            enter(t + 1)
        along_cols(t)
    for k in strips(W):
        at = pl.ds(k, STRIP)
        m_buf[at] = jnp.maximum(jnp.sqrt(m_buf[at]), 0.5)
    stores += fetch([(m_buf, mag)], sems.at[pl.ds(14, 1)])
    scale[...] = jnp.full(scale.shape, 1.0 / (jnp.max(g_buf[...]) + 1e-05), F32)
    for copy in stores:
        copy.wait()


def backward_kernel(
    offs_hbm, amp, far, mag, patch, probe, tables, grad, give, keep,
    offs, a_buf, m_buf, t_buf, f_buf, x_buf, p_buf, g_buf, q_buf, rows_in, cols_in, h_buf, sems,
):
    row, col, core = coords()
    order = [(t + 2 * (1 - core)) % MODES for t in range(MODES)]
    loads = fetch([(amp, a_buf), (tables.at[pl.ds(8, 2)], t_buf.at[pl.ds(8, 2)]), (mag, m_buf)], sems)
    t_loads = fetch([(tables.at[pl.ds(0, 4)], t_buf.at[pl.ds(0, 4)])], sems.at[pl.ds(19, 1)])
    f_loads = fetch([(far.at[order[0]], f_buf.at[0])], sems.at[pl.ds(3, 1)])
    loads[0].wait()
    loads[1].wait()
    x = a_buf[...]
    for turn in range(2):
        p1 = x.astype(BF)
        rest = x - p1.astype(F32)
        p2 = rest.astype(BF)
        p3 = (rest - p2.astype(F32)).astype(BF)
        if turn == 0:
            x = mm(t_buf[8], p1) + mm(t_buf[8], p2) + mm(t_buf[8], p3)
        else:
            x = mm(p1, t_buf[9]) + mm(p2, t_buf[9]) + mm(p3, t_buf[9])
    a_buf[...] = x
    loads[2].wait()
    f_loads[0].wait()
    t_loads += fetch([(tables.at[pl.ds(4, 4)], t_buf.at[pl.ds(4, 4)])], sems.at[pl.ds(20, 1)])
    loads += fetch([(patch, x_buf), (probe.at[order[0]], p_buf.at[0])], sems.at[pl.ds(4, 2)])
    f_loads += fetch([(far.at[order[t]], f_buf.at[t]) for t in range(1, MODES)], sems.at[pl.ds(6, MODES - 1)])
    p_loads = fetch([(probe.at[order[t]], p_buf.at[t]) for t in range(1, MODES)], sems.at[pl.ds(9, MODES - 1)])
    loads += fetch([(offs_hbm, offs)], sems.at[pl.ds(12, 1)])
    for k in strips(W):
        at = pl.ds(k, STRIP)
        m_buf[at] = a_buf[at] / m_buf[at] - 1.0

    def weigh(t):
        for k in strips(HALF):
            near, away = pl.ds(k, STRIP), pl.ds(HALF + k, STRIP)
            for p, at in ((0, near), (1, away)):
                put_split(cols_in.at[t, p], k, f_buf[t, p, near] * m_buf[at])
                put_split(cols_in.at[t, p], HALF + k, f_buf[t, p, away] * m_buf[at])

    def back_cols(t):
        h_buf[t, 0] = left(t_buf[0], t_buf[1], cols_in[t, 0])
        h_buf[t, 1] = left(t_buf[2], t_buf[3], cols_in[t, 1])
        for k in strips(HALF):
            near, away = pl.ds(k, STRIP), pl.ds(HALF + k, STRIP)
            u_re, v_re = h_buf[t, 0, near], h_buf[t, 1, near]
            u_im, v_im = h_buf[t, 0, away], h_buf[t, 1, away]
            for at, re, im in ((k, u_re + v_re, u_im + v_im), (HALF + k, u_re - v_re, u_im - v_im)):
                put_split(rows_in.at[t, 0], at, lanes(re[:, :HALF], im[:, :HALF]))
                put_split(rows_in.at[t, 1], at, lanes(re[:, HALF:], im[:, HALF:]))

    stores = []

    def back_rows(t):
        h_buf[t, 0] = right(rows_in[t, 0], t_buf[4], t_buf[5])
        h_buf[t, 1] = right(rows_in[t, 1], t_buf[6], t_buf[7])
        for k in strips(W):
            at = pl.ds(k, STRIP)
            u, v = h_buf[t, 0, at], h_buf[t, 1, at]
            add, sub = u + v, u - v
            b_re = lanes(add[:, :HALF], sub[:, :HALF])
            b_im = lanes(add[:, HALF:], sub[:, HALF:])
            p_re, p_im = p_buf[t, 0, at], p_buf[t, 1, at]
            o_re, o_im = x_buf[0, at], x_buf[1, at]
            g_re = p_re * b_re + p_im * b_im
            g_im = p_re * b_im - p_im * b_re
            g_buf[0, at] = g_re if t == 0 else g_buf[0, at] + g_re
            g_buf[1, at] = g_im if t == 0 else g_buf[1, at] + g_im
            q_buf[t, 0, at] = o_re * b_re + o_im * b_im
            q_buf[t, 1, at] = o_re * b_im - o_im * b_re
        target = give.at[t] if t < 2 else keep.at[t - 2]
        stores.extend(fetch([(q_buf.at[t], target)], sems.at[pl.ds(13 + t, 1)]))

    weigh(0)
    t_loads[0].wait()
    for t in range(MODES):
        back_cols(t)
        if t == 0:
            t_loads[1].wait()
            loads[3].wait()
            loads[4].wait()
        if t + 1 < MODES:
            f_loads[t + 1].wait()
            weigh(t + 1)
            p_loads[t].wait()
        back_rows(t)
    loads[5].wait()
    r, c = corner(offs, row, jnp.where(core == 0, col, col - 1))
    for i in range(2):
        g_buf[i] = pltpu.roll(pltpu.roll(g_buf[i], r % W, 0), c % W, 1)
        stores += fetch([(g_buf.at[i], grad.at[i])], sems.at[pl.ds(17 + i, 1)])
    for copy in stores:
        copy.wait()


def pick_kernel(owner_hbm, slots, out, owner, s_buf, o_buf, sems):
    row, col, core = coords()
    loads = fetch([(owner_hbm, owner), (slots, s_buf)], sems)
    loads[0].wait()
    base = row * NC
    owners = [owner[0, base + i] for i in range(NC)]
    index = []
    for i in range(NC):
        rank = jnp.int32(0)
        for q in range(i):
            rank = rank + jnp.where(owners[q] == owners[i], 1, 0)
        index.append(owners[i] * CAP + rank)
    loads[1].wait()
    for i in range(NC):
        device = jnp.where(core == 0, i, (i + 1) % NC)
        o_buf[device] = s_buf[index[i]]
    for copy in fetch([(o_buf, out)], sems.at[pl.ds(2, 1)]):
        copy.wait()


def sum_kernel(parts, out, p_buf, o_buf, sems):
    groups = 4
    per = 64 // groups
    loads = fetch(
        [(parts.at[pl.ds(g * per, per)], p_buf.at[pl.ds(g * per, per)]) for g in range(groups)], sems
    )
    total = jnp.zeros((16, W), F32)
    for g in range(groups):
        loads[g].wait()
        for n in range(per):
            total += p_buf[g * per + n]
    for n in range(8):
        o_buf[n] = total
    stores = fetch([(o_buf, out.at[pl.ds(8 * g, 8)]) for g in range(8)], sems.at[pl.ds(groups, 8)])
    for copy in stores:
        copy.wait()


def object_kernel(
    offs_hbm, scale, tile, own, got, above_first, above_second, out,
    offs, t_buf, w_buf, g_buf, f_buf, s_buf, o_buf, sems,
):
    row, col, core = coords()
    fetch([(offs_hbm, offs)], sems.at[pl.ds(12, 1)])[0].wait()
    loads = []
    for i in range(2):
        loads.append(
            fetch(
                [
                    (tile.at[i], t_buf.at[i]),
                    (own.at[i], w_buf.at[i]),
                    (got.at[i], g_buf.at[i]),
                    (above_first.at[i], f_buf.at[i]),
                    (above_second.at[i], s_buf.at[i]),
                ],
                sems.at[pl.ds(5 * i, 5)],
            )
        )
    a = iota((W, W), 0)
    b = iota((W, W), 1)
    s = scale[0, 0]
    r_s, c_s = corner(offs, row, col)
    r_b, c_b = corner(offs, row, col - 1)
    r_as, c_as = corner(offs, row - 1, col)
    r_ab, c_ab = corner(offs, row - 1, col - 1)

    def bands(at, v):
        return [v <= at, jnp.logical_and(v > at, v <= at + W)]

    even = core == 0
    rows_s, cols_s = bands(a, r_s), bands(b, c_s)
    rows_b = bands(a, r_b)
    in_b = c_b > b + W
    cols_as = bands(b, c_as)
    low_as = r_as > a + W
    low_ab = jnp.logical_and(r_ab > a + W, c_ab > b + W)
    stores = []
    for i in range(2):
        for copy in loads[i]:
            copy.wait()
        g_s = jnp.where(even, w_buf[i], g_buf[i])
        g_b = jnp.where(even, g_buf[i], w_buf[i])
        d_s = jnp.where(even, s_buf[i], f_buf[i])
        d_b = jnp.where(even, f_buf[i], s_buf[i])
        for p in range(2):
            for q in range(2):
                total = jnp.where(jnp.logical_and(rows_s[p], cols_s[q]), g_s, 0.0)
                if q == 0:
                    total += jnp.where(jnp.logical_and(rows_b[p], in_b), g_b, 0.0)
                if p == 0:
                    total += jnp.where(jnp.logical_and(low_as, cols_as[q]), d_s, 0.0)
                if p == 0 and q == 0:
                    total += jnp.where(low_ab, d_b, 0.0)
                at = (i, pl.ds(p * W, W), pl.ds(q * W, W))
                o_buf[at] = t_buf[at] + total * s
        stores += fetch([(o_buf.at[i], out.at[i])], sems.at[pl.ds(10 + i, 1)])
    for copy in stores:
        copy.wait()


def probe_kernel(first, probe, total, *refs):
    out, p_buf, m_buf, o_buf, sems = refs[-5:]
    core = lax.axis_index("core")
    base = 2 * jnp.where(first, core, 1 - core)
    loads = []
    for t in range(2):
        loads.append(
            fetch([(probe.at[base + t], p_buf.at[t]), (total.at[t], m_buf.at[t])], sems.at[pl.ds(2 * t, 2)])
        )
    stores = []
    for t in range(2):
        for copy in loads[t]:
            copy.wait()
        o_buf[t] = p_buf[t] + m_buf[t] * (1.0 / (NR * NC))
        stores += fetch([(o_buf.at[t], out.at[base + t])], sems.at[pl.ds(4 + t, 1)])
    for copy in stores:
        copy.wait()


SMEM = pl.BlockSpec(memory_space=pltpu.SMEM)
VMEM = pl.BlockSpec(memory_space=pltpu.VMEM)
HBM = pl.BlockSpec(memory_space=pltpu.HBM)
PIECE = (2, W, W)


def call(kernel, outs, ins, scratch, sems, *args, flops=0, data=0, out_specs=None, mb=62, alias=()):
    shapes = [jax.ShapeDtypeStruct(s, F32) for s in outs]
    buffers = [pltpu.VMEM(s, F32) if isinstance(s, tuple) else s for s in scratch]
    return pl.pallas_call(
        kernel,
        out_shape=shapes,
        in_specs=ins,
        out_specs=out_specs or [HBM] * len(outs),
        input_output_aliases=dict(alias),
        scratch_shapes=buffers + [pltpu.SemaphoreType.DMA((sems,))],
        compiler_params=pltpu.CompilerParams(vmem_limit_bytes=mb * 2**20),
        cost_estimate=pl.CostEstimate(flops=flops, bytes_accessed=data, transcendentals=0),
    )(*args)


def exchange(x):
    return lax.all_to_all(x, CHIPS, 0, 0, tiled=True)


def shards(tables, object_field, probe, measured, offsets, owner):
    offsets = offsets.T
    owner = owner.reshape(1, NR * NC)
    modes = (MODES, 2, W, W)
    half = (2, 2, W, W)
    split_buf = pltpu.VMEM((MODES, 2, 2, W, W), BF)
    table_buf = pltpu.VMEM(tables.shape, BF)
    offs_buf = pltpu.SMEM(offsets.shape, jnp.int32)
    owner_buf = pltpu.SMEM(owner.shape, jnp.int32)
    first, second = call(
        send_up_kernel, [PIECE] * 2, [HBM] * 2, [offs_buf, (2, W, TILE), PIECE, PIECE], 7,
        offsets, object_field, data=3 << 20,
    )
    below_first = lax.ppermute(first, ALL, UP)
    below = lax.ppermute(second, ALL, UP)
    side, own = call(
        send_side_kernel, [PIECE] * 2, [HBM] * 3, [offs_buf, (2, TILE, TILE), PIECE, PIECE, PIECE], 9,
        offsets, object_field, below_first, data=4 << 20, mb=54,
    )
    side = lax.ppermute(side, ALL, SIDE)
    spread = measured.reshape(CAP, NC, CHUNK, W).transpose(1, 0, 2, 3)
    spread = lax.all_to_all(spread, COL, 0, 0, tiled=True)
    slots = (NC * CAP, CHUNK, W)
    picked = call(
        pick_kernel, [(NC, CHUNK, W)], [HBM] * 2, [owner_buf, slots, (NC, CHUNK, W)], 3,
        owner, spread.reshape(slots), data=1 << 20, mb=50,
    )[0]
    amp = lax.all_to_all(picked, COL, 0, 0, tiled=True).reshape(W, W)
    far, mag, patch, scale = call(
        forward_kernel, [modes, (W, W), PIECE, (8, 128)], [HBM] * 6,
        [offs_buf, PIECE, PIECE, PIECE, modes, pltpu.VMEM((8, W, W), BF), modes, (W, W), PIECE, (W, W),
         split_buf, split_buf, modes], 16,
        offsets, own, below, side, probe, tables,
        flops=2 * 48 * W**3, data=8 << 20, out_specs=[HBM, HBM, HBM, VMEM], mb=50,
    )
    grad, give, keep = call(
        backward_kernel, [PIECE, half, half], [HBM] * 7,
        [offs_buf, (W, W), (W, W), table_buf, modes, PIECE, modes, PIECE, modes,
         split_buf, split_buf, modes], 21,
        offsets, amp, far, mag, patch, probe, tables,
        flops=2 * 48 * W**3, data=8 << 20, mb=49,
    )
    taken = lax.ppermute(give, ALL, SWAP)
    got = lax.ppermute(grad, ALL, back(SIDE))
    above_first = lax.ppermute(grad, ALL, back(UP))
    above_second = lax.ppermute(grad, ALL, back(SLANT))
    mine = (keep + taken).reshape(64, 16, W)
    inside = offsets[0, 0] >= 0
    parts = lax.cond(inside, exchange, jnp.zeros_like, mine)
    parts, got, above_first, above_second = lax.optimization_barrier((parts, got, above_first, above_second))
    copies = call(
        sum_kernel, [(64, 16, W)], [HBM], [(64, 16, W), (8, 16, W)], 12, parts, data=2 << 20, mb=50,
    )[0]
    mine = lax.all_to_all(copies, CHIPS, 0, 0, tiled=True)
    new_object = call(
        object_kernel, [(2, TILE, TILE)], [HBM, SMEM] + [HBM] * 5,
        [offs_buf, (2, TILE, TILE), PIECE, PIECE, PIECE, PIECE, (2, TILE, TILE)], 13,
        offsets, scale, object_field, grad, got, above_first, above_second, data=6 << 20,
    )[0]
    mine, new_object = lax.optimization_barrier((mine, new_object))
    mine = mine.reshape(half)
    theirs = lax.ppermute(mine, ALL, SWAP)
    new_probe = call(
        functools.partial(probe_kernel, True), [modes], [HBM] * 2, [half, half, half], 6,
        probe, mine, data=3 << 20, mb=50,
    )[0]
    new_probe = call(
        functools.partial(probe_kernel, False), [modes], [HBM] * 3, [half, half, half], 6,
        probe, theirs, new_probe, data=3 << 20, mb=50, alias=((2, 0),),
    )[0]
    return (new_object, new_probe)


def solution(mesh):
    inner = Mesh(mesh.devices.reshape(4, 2, 4, 4), ALL)
    tables = dft_tables()
    placed = (P(None, ("x", "core"), COL), P(), P(ALL, None, None), P(), P())

    def whole(*args):
        return shards(jnp.asarray(tables), *args)

    return jax.shard_map(
        whole, mesh=inner, in_specs=placed, out_specs=(P(None, ("x", "core"), COL), P()), check_vma=False
    )
```

```python
import functools
import math

import jax
import jax.numpy as jnp
import ml_dtypes
import numpy as np
from jax import lax
from jax.experimental import pallas as pl
from jax.experimental.pallas import tpu as pltpu
from jax.sharding import Mesh
from jax.sharding import PartitionSpec as P

W = 256
HALF = 128
TILE = 512
MODES = 4
CAP = 3
NR = 8
NC = 16
ALL = ("x", "core", "z", "y")
COL = ("z", "y")
CHIPS = ("x", "z", "y")
CHUNK = W // NC
BF = jnp.bfloat16
F32 = jnp.float32


def dft_tables():
    n = np.arange(HALF)[:, None]
    q = np.arange(HALF)[None, :]
    plain, turned = [], []
    for k in (2 * q, 2 * q + 1):
        angle = 2.0 * math.pi * ((n * k) % W) / W
        c = np.cos(angle) / math.sqrt(W)
        s = np.sin(angle) / math.sqrt(W)
        m = np.block([[c, -s], [s, c]])
        for t, out in ((m, plain), (m.T, turned)):
            hi = t.astype(ml_dtypes.bfloat16)
            lo = (t - hi.astype(np.float64)).astype(ml_dtypes.bfloat16)
            out += [hi, lo]
    out = plain + turned
    order = np.concatenate([np.arange(0, W, 2), np.arange(1, W, 2)])
    perm = np.zeros((W, W))
    perm[np.arange(W), order] = 1.0
    out += [perm.astype(ml_dtypes.bfloat16), perm.T.astype(ml_dtypes.bfloat16)]
    return np.stack(out)


def routes():
    up, side, slant, swap = [], [], [], []
    for r in range(NR):
        for c in range(NC):
            me = r * NC + c
            step = -1 if r % 2 == 0 else 1
            side.append((me, r * NC + (c + step) % NC))
            swap.append((me, (r ^ 1) * NC + c))
            above = (r - 1) % NR
            up.append((me, above * NC + c))
            slant.append((me, above * NC + (c - step) % NC))
    return up, side, slant, swap


def back(route):
    return [(b, a) for a, b in route]


UP, SIDE, SLANT, SWAP = routes()


def coords():
    core = lax.axis_index("core")
    row = lax.axis_index("x") * 2 + core
    col = lax.axis_index("z") * 4 + lax.axis_index("y")
    return row, col, core


def corner(offs, row, col):
    row = (row + NR) % NR
    col = (col + NC) % NC
    p = row * NC + col
    return offs[0, p] - row * TILE, offs[1, p] - col * TILE


def iota(shape, dim):
    return lax.broadcasted_iota(jnp.int32, shape, dim)


def fetch(pairs, sems):
    copies = []
    for n, (src, dst) in enumerate(pairs):
        copy = pltpu.make_async_copy(src, dst, sems.at[n])
        copy.start()
        copies.append(copy)
    return copies


def send_up_kernel(offs_hbm, tile, first, second, offs, t_buf, f_buf, s_buf, sems):
    row, col, core = coords()
    loads = fetch([(offs_hbm, offs)] + [(tile.at[i, pl.ds(0, W)], t_buf.at[i]) for i in range(2)], sems)
    loads[0].wait()
    _, c = corner(offs, row - 1, col)
    b = iota((W, W), 1)
    c1 = jnp.where(core == 1, 0, c)
    c2 = jnp.where(core == 1, c, 0)
    stores = []
    for i in range(2):
        loads[1 + i].wait()
        f_buf[i] = jnp.where(b >= c1, t_buf[i, :, :W], t_buf[i, :, W:])
        stores += fetch([(f_buf.at[i], first.at[i])], sems.at[pl.ds(3 + 2 * i, 1)])
        s_buf[i] = jnp.where(b >= c2, t_buf[i, :, :W], t_buf[i, :, W:])
        stores += fetch([(s_buf.at[i], second.at[i])], sems.at[pl.ds(4 + 2 * i, 1)])
    for copy in stores:
        copy.wait()


def send_side_kernel(offs_hbm, tile, below, side, own, offs, t_buf, b_buf, o_buf, w_buf, sems):
    row, col, core = coords()
    loads = fetch([(offs_hbm, offs)], sems)
    for i in range(2):
        loads += fetch([(tile.at[i], t_buf.at[i]), (below.at[i], b_buf.at[i])], sems.at[pl.ds(1 + 2 * i, 2)])
    loads[0].wait()
    even = core == 0
    r_s, c_s = corner(offs, row, col)
    r_b, _ = corner(offs, row, col - 1)
    r_side, c_side = jnp.where(even, r_b, r_s), jnp.where(even, 0, c_s)
    r_own, c_own = jnp.where(even, r_s, r_b), jnp.where(even, c_s, 0)
    a = iota((W, W), 0)
    b = iota((W, W), 1)
    stores = []
    for i in range(2):
        loads[1 + 2 * i].wait()
        loads[2 + 2 * i].wait()
        top = jnp.where(b >= c_side, t_buf[i, :W, :W], t_buf[i, :W, W:])
        low = jnp.where(b >= c_side, t_buf[i, W:, :W], t_buf[i, W:, W:])
        o_buf[i] = jnp.where(a >= r_side, top, jnp.where(a + W >= r_side, low, b_buf[i]))
        stores += fetch([(o_buf.at[i], side.at[i])], sems.at[pl.ds(5 + 2 * i, 1)])
        top = jnp.where(b >= c_own, t_buf[i, :W, :W], t_buf[i, :W, W:])
        low = jnp.where(b >= c_own, t_buf[i, W:, :W], t_buf[i, W:, W:])
        w_buf[i] = jnp.where(a >= r_own, top, low)
        stores += fetch([(w_buf.at[i], own.at[i])], sems.at[pl.ds(6 + 2 * i, 1)])
    for copy in stores:
        copy.wait()


def split(x):
    hi = x.astype(BF)
    lo = (x - hi.astype(F32)).astype(BF)
    return hi, lo


def mm(a, b):
    return jnp.dot(a, b, preferred_element_type=F32)


STRIP = 32


def strips(rows):
    return range(0, rows, STRIP)


def put_split(ref, at, x):
    hi, lo = split(x)
    ref[0, pl.ds(at, STRIP)] = hi
    ref[1, pl.ds(at, STRIP)] = lo


def right(x, hi, lo):
    return mm(jnp.concatenate([x[0], x[0], x[1]], axis=1), jnp.concatenate([hi, lo, hi], axis=0))


def left(hi, lo, x):
    return mm(jnp.concatenate([hi, lo, hi], axis=1), jnp.concatenate([x[0], x[0], x[1]], axis=0))


def lanes(a, b):
    return jnp.concatenate([a, b], axis=1)


def forward_kernel(
    offs_hbm, own, below, side, probe, tables, far, mag, patch, scale,
    offs, o_buf, b_buf, s_buf, p_buf, t_buf, f_buf, m_buf, x_buf, g_buf, rows_in, cols_in, h_buf, sems,
):
    row, col, core = coords()
    loads = fetch([(offs_hbm, offs), (own, o_buf), (below, b_buf), (side, s_buf)], sems)
    p_loads = fetch([(probe.at[0], p_buf.at[0])], sems.at[pl.ds(4, 1)])
    loads += fetch([(tables.at[pl.ds(0, 4)], t_buf.at[pl.ds(0, 4)])], sems.at[pl.ds(5, 1)])
    loads[0].wait()
    r, c = corner(offs, row, jnp.where(core == 0, col, col - 1))
    a = iota((W, W), 0)
    b = iota((W, W), 1)
    beyond = jnp.where(c > b + W, 1, 0)
    use_side = beyond != core
    row_shift = (2 * W - r) % W
    col_shift = (2 * W - c) % W
    for n in range(1, 4):
        loads[n].wait()
    loads += fetch([(tables.at[pl.ds(4, 4)], t_buf.at[pl.ds(4, 4)])], sems.at[pl.ds(15, 1)])
    p_loads += fetch([(probe.at[m], p_buf.at[m]) for m in range(1, MODES)], sems.at[pl.ds(6, MODES - 1)])
    for i in range(2):
        whole = jnp.where(use_side, s_buf[i], jnp.where(a + W >= r, o_buf[i], b_buf[i]))
        x_buf[i] = pltpu.roll(pltpu.roll(whole, row_shift, 0), col_shift, 1)

    stores = fetch([(x_buf, patch)], sems.at[pl.ds(9, 1)])

    def enter(t):
        p_loads[t].wait()
        for k in strips(W):
            at = pl.ds(k, STRIP)
            p_re, p_im = p_buf[t, 0, at], p_buf[t, 1, at]
            o_re, o_im = x_buf[0, at], x_buf[1, at]
            e_re = p_re * o_re - p_im * o_im
            e_im = p_re * o_im + p_im * o_re
            power = p_re * p_re + p_im * p_im
            g_buf[at] = power if t == 0 else g_buf[at] + power
            r0, r1 = e_re[:, :HALF], e_re[:, HALF:]
            i0, i1 = e_im[:, :HALF], e_im[:, HALF:]
            put_split(rows_in.at[t, 0], k, lanes(r0 + r1, i0 + i1))
            put_split(rows_in.at[t, 1], k, lanes(r0 - r1, i0 - i1))

    def along_rows(t):
        h_buf[t, 0] = right(rows_in[t, 0], t_buf[0], t_buf[1])
        h_buf[t, 1] = right(rows_in[t, 1], t_buf[2], t_buf[3])
        for k in strips(HALF):
            near, away = pl.ds(k, STRIP), pl.ds(HALF + k, STRIP)
            e0, e1 = h_buf[t, 0, near], h_buf[t, 0, away]
            o0, o1 = h_buf[t, 1, near], h_buf[t, 1, away]
            e_sum, e_dif, o_sum, o_dif = e0 + e1, e0 - e1, o0 + o1, o0 - o1
            put_split(cols_in.at[t, 0], k, lanes(e_sum[:, :HALF], o_sum[:, :HALF]))
            put_split(cols_in.at[t, 0], HALF + k, lanes(e_sum[:, HALF:], o_sum[:, HALF:]))
            put_split(cols_in.at[t, 1], k, lanes(e_dif[:, :HALF], o_dif[:, :HALF]))
            put_split(cols_in.at[t, 1], HALF + k, lanes(e_dif[:, HALF:], o_dif[:, HALF:]))

    def along_cols(t):
        f_buf[t, 0] = left(t_buf[4], t_buf[5], cols_in[t, 0])
        f_buf[t, 1] = left(t_buf[6], t_buf[7], cols_in[t, 1])
        stores.extend(fetch([(f_buf.at[t], far.at[t])], sems.at[pl.ds(10 + t, 1)]))
        for k in strips(HALF):
            near, away = pl.ds(k, STRIP), pl.ds(HALF + k, STRIP)
            for p, at in ((0, near), (1, away)):
                x, y = f_buf[t, p, near], f_buf[t, p, away]
                z = x * x + y * y
                m_buf[at] = z if t == 0 else m_buf[at] + z

    enter(0)
    loads[4].wait()
    loads[5].wait()
    for t in range(MODES):
        along_rows(t)
        if t + 1 < MODES:
            enter(t + 1)
        along_cols(t)
    for k in strips(W):
        at = pl.ds(k, STRIP)
        m_buf[at] = jnp.maximum(jnp.sqrt(m_buf[at]), 0.5)
    stores += fetch([(m_buf, mag)], sems.at[pl.ds(14, 1)])
    scale[...] = jnp.full(scale.shape, 1.0 / (jnp.max(g_buf[...]) + 1e-05), F32)
    for copy in stores:
        copy.wait()


def backward_kernel(
    offs_hbm, amp, far, mag, patch, probe, tables, grad, give, keep,
    offs, a_buf, m_buf, t_buf, f_buf, x_buf, p_buf, g_buf, q_buf, rows_in, cols_in, h_buf, sems,
):
    row, col, core = coords()
    order = [(t + 2 * (1 - core)) % MODES for t in range(MODES)]
    loads = fetch([(amp, a_buf), (tables.at[pl.ds(8, 2)], t_buf.at[pl.ds(8, 2)]), (mag, m_buf)], sems)
    t_loads = fetch([(tables.at[pl.ds(0, 4)], t_buf.at[pl.ds(0, 4)])], sems.at[pl.ds(19, 1)])
    f_loads = fetch([(far.at[order[0]], f_buf.at[0])], sems.at[pl.ds(3, 1)])
    loads[0].wait()
    loads[1].wait()
    x = a_buf[...]
    for turn in range(2):
        p1 = x.astype(BF)
        rest = x - p1.astype(F32)
        p2 = rest.astype(BF)
        p3 = (rest - p2.astype(F32)).astype(BF)
        if turn == 0:
            x = mm(t_buf[8], p1) + mm(t_buf[8], p2) + mm(t_buf[8], p3)
        else:
            x = mm(p1, t_buf[9]) + mm(p2, t_buf[9]) + mm(p3, t_buf[9])
    a_buf[...] = x
    loads[2].wait()
    f_loads[0].wait()
    t_loads += fetch([(tables.at[pl.ds(4, 4)], t_buf.at[pl.ds(4, 4)])], sems.at[pl.ds(20, 1)])
    loads += fetch([(patch, x_buf), (probe.at[order[0]], p_buf.at[0])], sems.at[pl.ds(4, 2)])
    f_loads += fetch([(far.at[order[t]], f_buf.at[t]) for t in range(1, MODES)], sems.at[pl.ds(6, MODES - 1)])
    p_loads = fetch([(probe.at[order[t]], p_buf.at[t]) for t in range(1, MODES)], sems.at[pl.ds(9, MODES - 1)])
    loads += fetch([(offs_hbm, offs)], sems.at[pl.ds(12, 1)])
    for k in strips(W):
        at = pl.ds(k, STRIP)
        m_buf[at] = a_buf[at] / m_buf[at] - 1.0

    def weigh(t):
        for k in strips(HALF):
            near, away = pl.ds(k, STRIP), pl.ds(HALF + k, STRIP)
            for p, at in ((0, near), (1, away)):
                put_split(cols_in.at[t, p], k, f_buf[t, p, near] * m_buf[at])
                put_split(cols_in.at[t, p], HALF + k, f_buf[t, p, away] * m_buf[at])

    def back_cols(t):
        h_buf[t, 0] = left(t_buf[0], t_buf[1], cols_in[t, 0])
        h_buf[t, 1] = left(t_buf[2], t_buf[3], cols_in[t, 1])
        for k in strips(HALF):
            near, away = pl.ds(k, STRIP), pl.ds(HALF + k, STRIP)
            u_re, v_re = h_buf[t, 0, near], h_buf[t, 1, near]
            u_im, v_im = h_buf[t, 0, away], h_buf[t, 1, away]
            for at, re, im in ((k, u_re + v_re, u_im + v_im), (HALF + k, u_re - v_re, u_im - v_im)):
                put_split(rows_in.at[t, 0], at, lanes(re[:, :HALF], im[:, :HALF]))
                put_split(rows_in.at[t, 1], at, lanes(re[:, HALF:], im[:, HALF:]))

    stores = []

    def back_rows(t):
        h_buf[t, 0] = right(rows_in[t, 0], t_buf[4], t_buf[5])
        h_buf[t, 1] = right(rows_in[t, 1], t_buf[6], t_buf[7])
        for k in strips(W):
            at = pl.ds(k, STRIP)
            u, v = h_buf[t, 0, at], h_buf[t, 1, at]
            add, sub = u + v, u - v
            b_re = lanes(add[:, :HALF], sub[:, :HALF])
            b_im = lanes(add[:, HALF:], sub[:, HALF:])
            p_re, p_im = p_buf[t, 0, at], p_buf[t, 1, at]
            o_re, o_im = x_buf[0, at], x_buf[1, at]
            g_re = p_re * b_re + p_im * b_im
            g_im = p_re * b_im - p_im * b_re
            g_buf[0, at] = g_re if t == 0 else g_buf[0, at] + g_re
            g_buf[1, at] = g_im if t == 0 else g_buf[1, at] + g_im
            q_buf[t, 0, at] = o_re * b_re + o_im * b_im
            q_buf[t, 1, at] = o_re * b_im - o_im * b_re
        target = give.at[t] if t < 2 else keep.at[t - 2]
        stores.extend(fetch([(q_buf.at[t], target)], sems.at[pl.ds(13 + t, 1)]))

    weigh(0)
    t_loads[0].wait()
    for t in range(MODES):
        back_cols(t)
        if t == 0:
            t_loads[1].wait()
            loads[3].wait()
            loads[4].wait()
        if t + 1 < MODES:
            f_loads[t + 1].wait()
            weigh(t + 1)
            p_loads[t].wait()
        back_rows(t)
    loads[5].wait()
    r, c = corner(offs, row, jnp.where(core == 0, col, col - 1))
    for i in range(2):
        g_buf[i] = pltpu.roll(pltpu.roll(g_buf[i], r % W, 0), c % W, 1)
        stores += fetch([(g_buf.at[i], grad.at[i])], sems.at[pl.ds(17 + i, 1)])
    for copy in stores:
        copy.wait()


def pick_kernel(owner_hbm, slots, out, owner, s_buf, o_buf, sems):
    row, col, core = coords()
    loads = fetch([(owner_hbm, owner), (slots, s_buf)], sems)
    loads[0].wait()
    base = row * NC
    owners = [owner[0, base + i] for i in range(NC)]
    index = []
    for i in range(NC):
        rank = jnp.int32(0)
        for q in range(i):
            rank = rank + jnp.where(owners[q] == owners[i], 1, 0)
        index.append(owners[i] * CAP + rank)
    loads[1].wait()
    for i in range(NC):
        device = jnp.where(core == 0, i, (i + 1) % NC)
        o_buf[device] = s_buf[index[i]]
    for copy in fetch([(o_buf, out)], sems.at[pl.ds(2, 1)]):
        copy.wait()


def sum_kernel(parts, out, p_buf, o_buf, sems):
    groups = 4
    per = 64 // groups
    loads = fetch(
        [(parts.at[pl.ds(g * per, per)], p_buf.at[pl.ds(g * per, per)]) for g in range(groups)], sems
    )
    total = jnp.zeros((16, W), F32)
    for g in range(groups):
        loads[g].wait()
        for n in range(per):
            total += p_buf[g * per + n]
    for n in range(8):
        o_buf[n] = total
    stores = fetch([(o_buf, out.at[pl.ds(8 * g, 8)]) for g in range(8)], sems.at[pl.ds(groups, 8)])
    for copy in stores:
        copy.wait()


def object_kernel(
    offs_hbm, scale, tile, own, got, above_first, above_second, out,
    offs, t_buf, w_buf, g_buf, f_buf, s_buf, o_buf, sems,
):
    row, col, core = coords()
    fetch([(offs_hbm, offs)], sems.at[pl.ds(12, 1)])[0].wait()
    loads = []
    for i in range(2):
        loads.append(
            fetch(
                [
                    (tile.at[i], t_buf.at[i]),
                    (own.at[i], w_buf.at[i]),
                    (got.at[i], g_buf.at[i]),
                    (above_first.at[i], f_buf.at[i]),
                    (above_second.at[i], s_buf.at[i]),
                ],
                sems.at[pl.ds(5 * i, 5)],
            )
        )
    a = iota((W, W), 0)
    b = iota((W, W), 1)
    s = scale[0, 0]
    r_s, c_s = corner(offs, row, col)
    r_b, c_b = corner(offs, row, col - 1)
    r_as, c_as = corner(offs, row - 1, col)
    r_ab, c_ab = corner(offs, row - 1, col - 1)

    def bands(at, v):
        return [v <= at, jnp.logical_and(v > at, v <= at + W)]

    even = core == 0
    rows_s, cols_s = bands(a, r_s), bands(b, c_s)
    rows_b = bands(a, r_b)
    in_b = c_b > b + W
    cols_as = bands(b, c_as)
    low_as = r_as > a + W
    low_ab = jnp.logical_and(r_ab > a + W, c_ab > b + W)
    stores = []
    for i in range(2):
        for copy in loads[i]:
            copy.wait()
        g_s = jnp.where(even, w_buf[i], g_buf[i])
        g_b = jnp.where(even, g_buf[i], w_buf[i])
        d_s = jnp.where(even, s_buf[i], f_buf[i])
        d_b = jnp.where(even, f_buf[i], s_buf[i])
        for p in range(2):
            for q in range(2):
                total = jnp.where(jnp.logical_and(rows_s[p], cols_s[q]), g_s, 0.0)
                if q == 0:
                    total += jnp.where(jnp.logical_and(rows_b[p], in_b), g_b, 0.0)
                if p == 0:
                    total += jnp.where(jnp.logical_and(low_as, cols_as[q]), d_s, 0.0)
                if p == 0 and q == 0:
                    total += jnp.where(low_ab, d_b, 0.0)
                at = (i, pl.ds(p * W, W), pl.ds(q * W, W))
                o_buf[at] = t_buf[at] + total * s
        stores += fetch([(o_buf.at[i], out.at[i])], sems.at[pl.ds(10 + i, 1)])
    for copy in stores:
        copy.wait()


def probe_kernel(first, probe, total, *refs):
    out, p_buf, m_buf, o_buf, sems = refs[-5:]
    core = lax.axis_index("core")
    base = 2 * jnp.where(first, core, 1 - core)
    loads = []
    for t in range(2):
        loads.append(
            fetch([(probe.at[base + t], p_buf.at[t]), (total.at[t], m_buf.at[t])], sems.at[pl.ds(2 * t, 2)])
        )
    stores = []
    for t in range(2):
        for copy in loads[t]:
            copy.wait()
        o_buf[t] = p_buf[t] + m_buf[t] * (1.0 / (NR * NC))
        stores += fetch([(o_buf.at[t], out.at[base + t])], sems.at[pl.ds(4 + t, 1)])
    for copy in stores:
        copy.wait()


SMEM = pl.BlockSpec(memory_space=pltpu.SMEM)
VMEM = pl.BlockSpec(memory_space=pltpu.VMEM)
HBM = pl.BlockSpec(memory_space=pltpu.HBM)
PIECE = (2, W, W)


def call(kernel, outs, ins, scratch, sems, *args, flops=0, data=0, out_specs=None, mb=62, alias=()):
    shapes = [jax.ShapeDtypeStruct(s, F32) for s in outs]
    buffers = [pltpu.VMEM(s, F32) if isinstance(s, tuple) else s for s in scratch]
    return pl.pallas_call(
        kernel,
        out_shape=shapes,
        in_specs=ins,
        out_specs=out_specs or [HBM] * len(outs),
        input_output_aliases=dict(alias),
        scratch_shapes=buffers + [pltpu.SemaphoreType.DMA((sems,))],
        compiler_params=pltpu.CompilerParams(vmem_limit_bytes=mb * 2**20),
        cost_estimate=pl.CostEstimate(flops=flops, bytes_accessed=data, transcendentals=0),
    )(*args)


def exchange(x):
    return lax.all_to_all(x, CHIPS, 0, 0, tiled=True)


def shards(tables, object_field, probe, measured, offsets, owner):
    offsets = offsets.T
    owner = owner.reshape(1, NR * NC)
    modes = (MODES, 2, W, W)
    half = (2, 2, W, W)
    split_buf = pltpu.VMEM((MODES, 2, 2, W, W), BF)
    table_buf = pltpu.VMEM(tables.shape, BF)
    offs_buf = pltpu.SMEM(offsets.shape, jnp.int32)
    owner_buf = pltpu.SMEM(owner.shape, jnp.int32)
    first, second = call(
        send_up_kernel, [PIECE] * 2, [HBM] * 2, [offs_buf, (2, W, TILE), PIECE, PIECE], 7,
        offsets, object_field, data=3 << 20,
    )
    below_first = lax.ppermute(first, ALL, UP)
    below = lax.ppermute(second, ALL, UP)
    side, own = call(
        send_side_kernel, [PIECE] * 2, [HBM] * 3, [offs_buf, (2, TILE, TILE), PIECE, PIECE, PIECE], 9,
        offsets, object_field, below_first, data=4 << 20, mb=54,
    )
    side = lax.ppermute(side, ALL, SIDE)
    spread = measured.reshape(CAP, NC, CHUNK, W).transpose(1, 0, 2, 3)
    spread = lax.all_to_all(spread, COL, 0, 0, tiled=True)
    slots = (NC * CAP, CHUNK, W)
    picked = call(
        pick_kernel, [(NC, CHUNK, W)], [HBM] * 2, [owner_buf, slots, (NC, CHUNK, W)], 3,
        owner, spread.reshape(slots), data=1 << 20, mb=50,
    )[0]
    amp = lax.all_to_all(picked, COL, 0, 0, tiled=True).reshape(W, W)
    far, mag, patch, scale = call(
        forward_kernel, [modes, (W, W), PIECE, (8, 128)], [HBM] * 6,
        [offs_buf, PIECE, PIECE, PIECE, modes, pltpu.VMEM((8, W, W), BF), modes, (W, W), PIECE, (W, W),
         split_buf, split_buf, modes], 16,
        offsets, own, below, side, probe, tables,
        flops=2 * 48 * W**3, data=8 << 20, out_specs=[HBM, HBM, HBM, VMEM], mb=50,
    )
    grad, give, keep = call(
        backward_kernel, [PIECE, half, half], [HBM] * 7,
        [offs_buf, (W, W), (W, W), table_buf, modes, PIECE, modes, PIECE, modes,
         split_buf, split_buf, modes], 21,
        offsets, amp, far, mag, patch, probe, tables,
        flops=2 * 48 * W**3, data=8 << 20, mb=49,
    )
    taken = lax.ppermute(give, ALL, SWAP)
    got = lax.ppermute(grad, ALL, back(SIDE))
    above_first = lax.ppermute(grad, ALL, back(UP))
    above_second = lax.ppermute(grad, ALL, back(SLANT))
    mine = (keep + taken).reshape(64, 16, W)
    inside = offsets[0, 0] >= 0
    parts = lax.cond(inside, exchange, jnp.zeros_like, mine)
    parts, got, above_first, above_second = lax.optimization_barrier((parts, got, above_first, above_second))
    copies = call(
        sum_kernel, [(64, 16, W)], [HBM], [(64, 16, W), (8, 16, W)], 12, parts, data=2 << 20, mb=50,
    )[0]
    mine = lax.all_to_all(copies, CHIPS, 0, 0, tiled=True)
    new_object = call(
        object_kernel, [(2, TILE, TILE)], [HBM, SMEM] + [HBM] * 5,
        [offs_buf, (2, TILE, TILE), PIECE, PIECE, PIECE, PIECE, (2, TILE, TILE)], 13,
        offsets, scale, object_field, grad, got, above_first, above_second, data=6 << 20,
    )[0]
    mine, new_object = lax.optimization_barrier((mine, new_object))
    mine = mine.reshape(half)
    theirs = lax.ppermute(mine, ALL, SWAP)
    new_probe = call(
        functools.partial(probe_kernel, True), [modes], [HBM] * 2, [half, half, half], 6,
        probe, mine, data=3 << 20, mb=50,
    )[0]
    new_probe = call(
        functools.partial(probe_kernel, False), [modes], [HBM] * 3, [half, half, half], 6,
        probe, theirs, new_probe, data=3 << 20, mb=50, alias=((2, 0),),
    )[0]
    return (new_object, new_probe)


def solution(mesh):
    inner = Mesh(mesh.devices.reshape(4, 2, 4, 4), ALL)
    tables = dft_tables()
    placed = (P(None, ("x", "core"), COL), P(), P(ALL, None, None), P(), P())

    def whole(*args):
        return shards(jnp.asarray(tables), *args)

    return jax.shard_map(
        whole, mesh=inner, in_specs=placed, out_specs=(P(None, ("x", "core"), COL), P()), check_vma=False
    )
```

```python
import functools
import math

import jax
import jax.numpy as jnp
import ml_dtypes
import numpy as np
from jax import lax
from jax.experimental import pallas as pl
from jax.experimental.pallas import tpu as pltpu
from jax.sharding import Mesh
from jax.sharding import PartitionSpec as P

W = 256
HALF = 128
TILE = 512
MODES = 4
CAP = 3
NR = 8
NC = 16
ALL = ("x", "core", "z", "y")
COL = ("z", "y")
CHIPS = ("x", "z", "y")
CHUNK = W // NC
BF = jnp.bfloat16
F32 = jnp.float32


def dft_tables():
    n = np.arange(HALF)[:, None]
    q = np.arange(HALF)[None, :]
    plain, turned = [], []
    for k in (2 * q, 2 * q + 1):
        angle = 2.0 * math.pi * ((n * k) % W) / W
        c = np.cos(angle) / math.sqrt(W)
        s = np.sin(angle) / math.sqrt(W)
        m = np.block([[c, -s], [s, c]])
        for t, out in ((m, plain), (m.T, turned)):
            hi = t.astype(ml_dtypes.bfloat16)
            lo = (t - hi.astype(np.float64)).astype(ml_dtypes.bfloat16)
            out += [hi, lo]
    out = plain + turned
    order = np.concatenate([np.arange(0, W, 2), np.arange(1, W, 2)])
    perm = np.zeros((W, W))
    perm[np.arange(W), order] = 1.0
    out += [perm.astype(ml_dtypes.bfloat16), perm.T.astype(ml_dtypes.bfloat16)]
    return np.stack(out)


def routes():
    up, side, slant, swap = [], [], [], []
    for r in range(NR):
        for c in range(NC):
            me = r * NC + c
            step = -1 if r % 2 == 0 else 1
            side.append((me, r * NC + (c + step) % NC))
            swap.append((me, (r ^ 1) * NC + c))
            above = (r - 1) % NR
            up.append((me, above * NC + c))
            slant.append((me, above * NC + (c - step) % NC))
    return up, side, slant, swap


def back(route):
    return [(b, a) for a, b in route]


UP, SIDE, SLANT, SWAP = routes()


def coords():
    core = lax.axis_index("core")
    row = lax.axis_index("x") * 2 + core
    col = lax.axis_index("z") * 4 + lax.axis_index("y")
    return row, col, core


def corner(offs, row, col):
    row = (row + NR) % NR
    col = (col + NC) % NC
    p = row * NC + col
    return offs[0, p] - row * TILE, offs[1, p] - col * TILE


def iota(shape, dim):
    return lax.broadcasted_iota(jnp.int32, shape, dim)


def fetch(pairs, sems):
    copies = []
    for n, (src, dst) in enumerate(pairs):
        copy = pltpu.make_async_copy(src, dst, sems.at[n])
        copy.start()
        copies.append(copy)
    return copies


def send_up_kernel(offs_hbm, tile, first, offs, t_buf, f_buf, sems):
    row, col, core = coords()
    loads = fetch([(offs_hbm, offs)] + [(tile.at[i, pl.ds(0, W)], t_buf.at[i]) for i in range(2)], sems)
    loads[0].wait()
    _, c = corner(offs, row - 1, col)
    b = iota((W, W), 1)
    c1 = jnp.where(core == 1, 0, c)
    stores = []
    for i in range(2):
        loads[1 + i].wait()
        f_buf[i] = jnp.where(b >= c1, t_buf[i, :, :W], t_buf[i, :, W:])
        stores += fetch([(f_buf.at[i], first.at[i])], sems.at[pl.ds(3 + i, 1)])
    for copy in stores:
        copy.wait()


def send_side_kernel(offs_hbm, tile, below, side, own, second, offs, t_buf, b_buf, o_buf, w_buf, u_buf, sems):
    row, col, core = coords()
    loads = fetch([(offs_hbm, offs)], sems)
    for i in range(2):
        loads += fetch([(tile.at[i], t_buf.at[i]), (below.at[i], b_buf.at[i])], sems.at[pl.ds(1 + 2 * i, 2)])
    loads[0].wait()
    even = core == 0
    r_s, c_s = corner(offs, row, col)
    r_b, _ = corner(offs, row, col - 1)
    _, c_up = corner(offs, row - 1, col)
    c_up = jnp.where(even, 0, c_up)
    r_side, c_side = jnp.where(even, r_b, r_s), jnp.where(even, 0, c_s)
    r_own, c_own = jnp.where(even, r_s, r_b), jnp.where(even, c_s, 0)
    a = iota((W, W), 0)
    b = iota((W, W), 1)
    stores = []
    for i in range(2):
        loads[1 + 2 * i].wait()
        loads[2 + 2 * i].wait()
        top = jnp.where(b >= c_side, t_buf[i, :W, :W], t_buf[i, :W, W:])
        low = jnp.where(b >= c_side, t_buf[i, W:, :W], t_buf[i, W:, W:])
        o_buf[i] = jnp.where(a >= r_side, top, jnp.where(a + W >= r_side, low, b_buf[i]))
        stores += fetch([(o_buf.at[i], side.at[i])], sems.at[pl.ds(5 + 2 * i, 1)])
        top = jnp.where(b >= c_own, t_buf[i, :W, :W], t_buf[i, :W, W:])
        low = jnp.where(b >= c_own, t_buf[i, W:, :W], t_buf[i, W:, W:])
        w_buf[i] = jnp.where(a >= r_own, top, low)
        stores += fetch([(w_buf.at[i], own.at[i])], sems.at[pl.ds(6 + 2 * i, 1)])
        u_buf[i] = jnp.where(b >= c_up, t_buf[i, :W, :W], t_buf[i, :W, W:])
        stores += fetch([(u_buf.at[i], second.at[i])], sems.at[pl.ds(9 + i, 1)])
    for copy in stores:
        copy.wait()


def split(x):
    hi = x.astype(BF)
    lo = (x - hi.astype(F32)).astype(BF)
    return hi, lo


def mm(a, b):
    return jnp.dot(a, b, preferred_element_type=F32)


STRIP = 32


def strips(rows):
    return range(0, rows, STRIP)


def put_split(ref, at, x):
    hi, lo = split(x)
    ref[0, pl.ds(at, STRIP)] = hi
    ref[1, pl.ds(at, STRIP)] = lo


def right(x, hi, lo):
    return mm(jnp.concatenate([x[0], x[0], x[1]], axis=1), jnp.concatenate([hi, lo, hi], axis=0))


def left(hi, lo, x):
    return mm(jnp.concatenate([hi, lo, hi], axis=1), jnp.concatenate([x[0], x[0], x[1]], axis=0))


def lanes(a, b):
    return jnp.concatenate([a, b], axis=1)


def forward_kernel(
    offs_hbm, own, below, side, probe, tables, far, mag, patch, scale,
    offs, o_buf, b_buf, s_buf, p_buf, t_buf, f_buf, m_buf, x_buf, g_buf, rows_in, cols_in, h_buf, sems,
):
    row, col, core = coords()
    loads = fetch([(offs_hbm, offs), (own, o_buf), (below, b_buf), (side, s_buf)], sems)
    p_loads = fetch([(probe.at[0], p_buf.at[0])], sems.at[pl.ds(4, 1)])
    loads += fetch([(tables.at[pl.ds(0, 4)], t_buf.at[pl.ds(0, 4)])], sems.at[pl.ds(5, 1)])
    loads[0].wait()
    r, c = corner(offs, row, jnp.where(core == 0, col, col - 1))
    a = iota((W, W), 0)
    b = iota((W, W), 1)
    beyond = jnp.where(c > b + W, 1, 0)
    use_side = beyond != core
    row_shift = (2 * W - r) % W
    col_shift = (2 * W - c) % W
    for n in range(1, 4):
        loads[n].wait()
    loads += fetch([(tables.at[pl.ds(4, 4)], t_buf.at[pl.ds(4, 4)])], sems.at[pl.ds(15, 1)])
    p_loads += fetch([(probe.at[m], p_buf.at[m]) for m in range(1, MODES)], sems.at[pl.ds(6, MODES - 1)])
    for i in range(2):
        whole = jnp.where(use_side, s_buf[i], jnp.where(a + W >= r, o_buf[i], b_buf[i]))
        x_buf[i] = pltpu.roll(pltpu.roll(whole, row_shift, 0), col_shift, 1)

    stores = fetch([(x_buf, patch)], sems.at[pl.ds(9, 1)])

    def enter(t):
        p_loads[t].wait()
        for k in strips(W):
            at = pl.ds(k, STRIP)
            p_re, p_im = p_buf[t, 0, at], p_buf[t, 1, at]
            o_re, o_im = x_buf[0, at], x_buf[1, at]
            e_re = p_re * o_re - p_im * o_im
            e_im = p_re * o_im + p_im * o_re
            power = p_re * p_re + p_im * p_im
            g_buf[at] = power if t == 0 else g_buf[at] + power
            r0, r1 = e_re[:, :HALF], e_re[:, HALF:]
            i0, i1 = e_im[:, :HALF], e_im[:, HALF:]
            put_split(rows_in.at[t, 0], k, lanes(r0 + r1, i0 + i1))
            put_split(rows_in.at[t, 1], k, lanes(r0 - r1, i0 - i1))

    def along_rows(t):
        h_buf[t, 0] = right(rows_in[t, 0], t_buf[0], t_buf[1])
        h_buf[t, 1] = right(rows_in[t, 1], t_buf[2], t_buf[3])
        for k in strips(HALF):
            near, away = pl.ds(k, STRIP), pl.ds(HALF + k, STRIP)
            e0, e1 = h_buf[t, 0, near], h_buf[t, 0, away]
            o0, o1 = h_buf[t, 1, near], h_buf[t, 1, away]
            e_sum, e_dif, o_sum, o_dif = e0 + e1, e0 - e1, o0 + o1, o0 - o1
            put_split(cols_in.at[t, 0], k, lanes(e_sum[:, :HALF], o_sum[:, :HALF]))
            put_split(cols_in.at[t, 0], HALF + k, lanes(e_sum[:, HALF:], o_sum[:, HALF:]))
            put_split(cols_in.at[t, 1], k, lanes(e_dif[:, :HALF], o_dif[:, :HALF]))
            put_split(cols_in.at[t, 1], HALF + k, lanes(e_dif[:, HALF:], o_dif[:, HALF:]))

    def along_cols(t):
        f_buf[t, 0] = left(t_buf[4], t_buf[5], cols_in[t, 0])
        f_buf[t, 1] = left(t_buf[6], t_buf[7], cols_in[t, 1])
        stores.extend(fetch([(f_buf.at[t], far.at[t])], sems.at[pl.ds(10 + t, 1)]))
        for k in strips(HALF):
            near, away = pl.ds(k, STRIP), pl.ds(HALF + k, STRIP)
            for p, at in ((0, near), (1, away)):
                x, y = f_buf[t, p, near], f_buf[t, p, away]
                z = x * x + y * y
                m_buf[at] = z if t == 0 else m_buf[at] + z

    enter(0)
    loads[4].wait()
    loads[5].wait()
    for t in range(MODES):
        along_rows(t)
        if t + 1 < MODES:
            enter(t + 1)
        along_cols(t)
    for k in strips(W):
        at = pl.ds(k, STRIP)
        m_buf[at] = jnp.maximum(jnp.sqrt(m_buf[at]), 0.5)
    stores += fetch([(m_buf, mag)], sems.at[pl.ds(14, 1)])
    scale[...] = jnp.full(scale.shape, 1.0 / (jnp.max(g_buf[...]) + 1e-05), F32)
    for copy in stores:
        copy.wait()


def backward_kernel(
    offs_hbm, amp, far, mag, patch, probe, tables, grad, give, keep,
    offs, a_buf, m_buf, t_buf, f_buf, x_buf, p_buf, g_buf, q_buf, rows_in, cols_in, h_buf, sems,
):
    row, col, core = coords()
    order = [(t + 2 * (1 - core)) % MODES for t in range(MODES)]
    loads = fetch([(amp, a_buf), (tables.at[pl.ds(8, 2)], t_buf.at[pl.ds(8, 2)]), (mag, m_buf)], sems)
    t_loads = fetch([(tables.at[pl.ds(0, 4)], t_buf.at[pl.ds(0, 4)])], sems.at[pl.ds(19, 1)])
    f_loads = fetch([(far.at[order[0]], f_buf.at[0])], sems.at[pl.ds(3, 1)])
    loads[0].wait()
    loads[1].wait()
    x = a_buf[...]
    for turn in range(2):
        p1 = x.astype(BF)
        rest = x - p1.astype(F32)
        p2 = rest.astype(BF)
        p3 = (rest - p2.astype(F32)).astype(BF)
        if turn == 0:
            x = mm(t_buf[8], p1) + mm(t_buf[8], p2) + mm(t_buf[8], p3)
        else:
            x = mm(p1, t_buf[9]) + mm(p2, t_buf[9]) + mm(p3, t_buf[9])
    a_buf[...] = x
    loads[2].wait()
    f_loads[0].wait()
    t_loads += fetch([(tables.at[pl.ds(4, 4)], t_buf.at[pl.ds(4, 4)])], sems.at[pl.ds(20, 1)])
    loads += fetch([(patch, x_buf), (probe.at[order[0]], p_buf.at[0])], sems.at[pl.ds(4, 2)])
    f_loads += fetch([(far.at[order[t]], f_buf.at[t]) for t in range(1, MODES)], sems.at[pl.ds(6, MODES - 1)])
    p_loads = fetch([(probe.at[order[t]], p_buf.at[t]) for t in range(1, MODES)], sems.at[pl.ds(9, MODES - 1)])
    loads += fetch([(offs_hbm, offs)], sems.at[pl.ds(12, 1)])
    for k in strips(W):
        at = pl.ds(k, STRIP)
        m_buf[at] = a_buf[at] / m_buf[at] - 1.0

    def weigh(t):
        for k in strips(HALF):
            near, away = pl.ds(k, STRIP), pl.ds(HALF + k, STRIP)
            for p, at in ((0, near), (1, away)):
                put_split(cols_in.at[t, p], k, f_buf[t, p, near] * m_buf[at])
                put_split(cols_in.at[t, p], HALF + k, f_buf[t, p, away] * m_buf[at])

    def back_cols(t):
        h_buf[t, 0] = left(t_buf[0], t_buf[1], cols_in[t, 0])
        h_buf[t, 1] = left(t_buf[2], t_buf[3], cols_in[t, 1])
        for k in strips(HALF):
            near, away = pl.ds(k, STRIP), pl.ds(HALF + k, STRIP)
            u_re, v_re = h_buf[t, 0, near], h_buf[t, 1, near]
            u_im, v_im = h_buf[t, 0, away], h_buf[t, 1, away]
            for at, re, im in ((k, u_re + v_re, u_im + v_im), (HALF + k, u_re - v_re, u_im - v_im)):
                put_split(rows_in.at[t, 0], at, lanes(re[:, :HALF], im[:, :HALF]))
                put_split(rows_in.at[t, 1], at, lanes(re[:, HALF:], im[:, HALF:]))

    stores = []

    def back_rows(t):
        h_buf[t, 0] = right(rows_in[t, 0], t_buf[4], t_buf[5])
        h_buf[t, 1] = right(rows_in[t, 1], t_buf[6], t_buf[7])
        for k in strips(W):
            at = pl.ds(k, STRIP)
            u, v = h_buf[t, 0, at], h_buf[t, 1, at]
            add, sub = u + v, u - v
            b_re = lanes(add[:, :HALF], sub[:, :HALF])
            b_im = lanes(add[:, HALF:], sub[:, HALF:])
            p_re, p_im = p_buf[t, 0, at], p_buf[t, 1, at]
            o_re, o_im = x_buf[0, at], x_buf[1, at]
            g_re = p_re * b_re + p_im * b_im
            g_im = p_re * b_im - p_im * b_re
            g_buf[0, at] = g_re if t == 0 else g_buf[0, at] + g_re
            g_buf[1, at] = g_im if t == 0 else g_buf[1, at] + g_im
            q_buf[t, 0, at] = o_re * b_re + o_im * b_im
            q_buf[t, 1, at] = o_re * b_im - o_im * b_re
        target = give.at[t] if t < 2 else keep.at[t - 2]
        stores.extend(fetch([(q_buf.at[t], target)], sems.at[pl.ds(13 + t, 1)]))

    weigh(0)
    t_loads[0].wait()
    for t in range(MODES):
        back_cols(t)
        if t == 0:
            t_loads[1].wait()
            loads[3].wait()
            loads[4].wait()
        if t + 1 < MODES:
            f_loads[t + 1].wait()
            weigh(t + 1)
            p_loads[t].wait()
        back_rows(t)
    loads[5].wait()
    r, c = corner(offs, row, jnp.where(core == 0, col, col - 1))
    for i in range(2):
        g_buf[i] = pltpu.roll(pltpu.roll(g_buf[i], r % W, 0), c % W, 1)
        stores += fetch([(g_buf.at[i], grad.at[i])], sems.at[pl.ds(17 + i, 1)])
    for copy in stores:
        copy.wait()


def pick_kernel(owner_hbm, slots, out, owner, s_buf, o_buf, sems):
    row, col, core = coords()
    loads = fetch([(owner_hbm, owner), (slots, s_buf)], sems)
    loads[0].wait()
    base = row * NC
    owners = [owner[0, base + i] for i in range(NC)]
    index = []
    for i in range(NC):
        rank = jnp.int32(0)
        for q in range(i):
            rank = rank + jnp.where(owners[q] == owners[i], 1, 0)
        index.append(owners[i] * CAP + rank)
    loads[1].wait()
    for i in range(NC):
        device = jnp.where(core == 0, i, (i + 1) % NC)
        o_buf[device] = s_buf[index[i]]
    for copy in fetch([(o_buf, out)], sems.at[pl.ds(2, 1)]):
        copy.wait()


def sum_kernel(parts, out, p_buf, o_buf, sems):
    groups = 4
    per = 64 // groups
    loads = fetch(
        [(parts.at[pl.ds(g * per, per)], p_buf.at[pl.ds(g * per, per)]) for g in range(groups)], sems
    )
    total = jnp.zeros((16, W), F32)
    for g in range(groups):
        loads[g].wait()
        for n in range(per):
            total += p_buf[g * per + n]
    for n in range(8):
        o_buf[n] = total
    stores = fetch([(o_buf, out.at[pl.ds(8 * g, 8)]) for g in range(8)], sems.at[pl.ds(groups, 8)])
    for copy in stores:
        copy.wait()


def object_kernel(
    offs_hbm, scale, tile, own, got, above_first, above_second, out,
    offs, t_buf, w_buf, g_buf, f_buf, s_buf, o_buf, sems,
):
    row, col, core = coords()
    fetch([(offs_hbm, offs)], sems.at[pl.ds(12, 1)])[0].wait()
    loads = []
    for i in range(2):
        loads.append(
            fetch(
                [
                    (tile.at[i], t_buf.at[i]),
                    (own.at[i], w_buf.at[i]),
                    (got.at[i], g_buf.at[i]),
                    (above_first.at[i], f_buf.at[i]),
                    (above_second.at[i], s_buf.at[i]),
                ],
                sems.at[pl.ds(5 * i, 5)],
            )
        )
    a = iota((W, W), 0)
    b = iota((W, W), 1)
    s = scale[0, 0]
    r_s, c_s = corner(offs, row, col)
    r_b, c_b = corner(offs, row, col - 1)
    r_as, c_as = corner(offs, row - 1, col)
    r_ab, c_ab = corner(offs, row - 1, col - 1)

    def bands(at, v):
        return [v <= at, jnp.logical_and(v > at, v <= at + W)]

    even = core == 0
    rows_s, cols_s = bands(a, r_s), bands(b, c_s)
    rows_b = bands(a, r_b)
    in_b = c_b > b + W
    cols_as = bands(b, c_as)
    low_as = r_as > a + W
    low_ab = jnp.logical_and(r_ab > a + W, c_ab > b + W)
    stores = []
    for i in range(2):
        for copy in loads[i]:
            copy.wait()
        g_s = jnp.where(even, w_buf[i], g_buf[i])
        g_b = jnp.where(even, g_buf[i], w_buf[i])
        d_s = jnp.where(even, s_buf[i], f_buf[i])
        d_b = jnp.where(even, f_buf[i], s_buf[i])
        for p in range(2):
            for q in range(2):
                total = jnp.where(jnp.logical_and(rows_s[p], cols_s[q]), g_s, 0.0)
                if q == 0:
                    total += jnp.where(jnp.logical_and(rows_b[p], in_b), g_b, 0.0)
                if p == 0:
                    total += jnp.where(jnp.logical_and(low_as, cols_as[q]), d_s, 0.0)
                if p == 0 and q == 0:
                    total += jnp.where(low_ab, d_b, 0.0)
                at = (i, pl.ds(p * W, W), pl.ds(q * W, W))
                o_buf[at] = t_buf[at] + total * s
        stores += fetch([(o_buf.at[i], out.at[i])], sems.at[pl.ds(10 + i, 1)])
    for copy in stores:
        copy.wait()


def probe_kernel(first, probe, total, *refs):
    out, p_buf, m_buf, o_buf, sems = refs[-5:]
    core = lax.axis_index("core")
    base = 2 * jnp.where(first, core, 1 - core)
    loads = []
    for t in range(2):
        loads.append(
            fetch([(probe.at[base + t], p_buf.at[t]), (total.at[t], m_buf.at[t])], sems.at[pl.ds(2 * t, 2)])
        )
    stores = []
    for t in range(2):
        for copy in loads[t]:
            copy.wait()
        o_buf[t] = p_buf[t] + m_buf[t] * (1.0 / (NR * NC))
        stores += fetch([(o_buf.at[t], out.at[base + t])], sems.at[pl.ds(4 + t, 1)])
    for copy in stores:
        copy.wait()


SMEM = pl.BlockSpec(memory_space=pltpu.SMEM)
VMEM = pl.BlockSpec(memory_space=pltpu.VMEM)
HBM = pl.BlockSpec(memory_space=pltpu.HBM)
PIECE = (2, W, W)


def call(kernel, outs, ins, scratch, sems, *args, flops=0, data=0, out_specs=None, mb=62, alias=()):
    shapes = [jax.ShapeDtypeStruct(s, F32) for s in outs]
    buffers = [pltpu.VMEM(s, F32) if isinstance(s, tuple) else s for s in scratch]
    return pl.pallas_call(
        kernel,
        out_shape=shapes,
        in_specs=ins,
        out_specs=out_specs or [HBM] * len(outs),
        input_output_aliases=dict(alias),
        scratch_shapes=buffers + [pltpu.SemaphoreType.DMA((sems,))],
        compiler_params=pltpu.CompilerParams(vmem_limit_bytes=mb * 2**20),
        cost_estimate=pl.CostEstimate(flops=flops, bytes_accessed=data, transcendentals=0),
    )(*args)


def exchange(x):
    return lax.all_to_all(x, CHIPS, 0, 0, tiled=True)


def shards(tables, object_field, probe, measured, offsets, owner):
    offsets = offsets.T
    owner = owner.reshape(1, NR * NC)
    modes = (MODES, 2, W, W)
    half = (2, 2, W, W)
    split_buf = pltpu.VMEM((MODES, 2, 2, W, W), BF)
    table_buf = pltpu.VMEM(tables.shape, BF)
    offs_buf = pltpu.SMEM(offsets.shape, jnp.int32)
    owner_buf = pltpu.SMEM(owner.shape, jnp.int32)
    first = call(
        send_up_kernel, [PIECE], [HBM] * 2, [offs_buf, (2, W, TILE), PIECE], 5,
        offsets, object_field, data=3 << 20,
    )[0]
    below_first = lax.ppermute(first, ALL, UP)
    side, own, second = call(
        send_side_kernel, [PIECE] * 3, [HBM] * 3, [offs_buf, (2, TILE, TILE), PIECE, PIECE, PIECE, PIECE], 11,
        offsets, object_field, below_first, data=4 << 20, mb=54,
    )
    side = lax.ppermute(side, ALL, SIDE)
    below = lax.ppermute(second, ALL, UP)
    spread = measured.reshape(CAP, NC, CHUNK, W).transpose(1, 0, 2, 3)
    spread = lax.all_to_all(spread, COL, 0, 0, tiled=True)
    slots = (NC * CAP, CHUNK, W)
    picked = call(
        pick_kernel, [(NC, CHUNK, W)], [HBM] * 2, [owner_buf, slots, (NC, CHUNK, W)], 3,
        owner, spread.reshape(slots), data=1 << 20, mb=50,
    )[0]
    amp = lax.all_to_all(picked, COL, 0, 0, tiled=True).reshape(W, W)
    far, mag, patch, scale = call(
        forward_kernel, [modes, (W, W), PIECE, (8, 128)], [HBM] * 6,
        [offs_buf, PIECE, PIECE, PIECE, modes, pltpu.VMEM((8, W, W), BF), modes, (W, W), PIECE, (W, W),
         split_buf, split_buf, modes], 16,
        offsets, own, below, side, probe, tables,
        flops=2 * 48 * W**3, data=8 << 20, out_specs=[HBM, HBM, HBM, VMEM], mb=50,
    )
    grad, give, keep = call(
        backward_kernel, [PIECE, half, half], [HBM] * 7,
        [offs_buf, (W, W), (W, W), table_buf, modes, PIECE, modes, PIECE, modes,
         split_buf, split_buf, modes], 21,
        offsets, amp, far, mag, patch, probe, tables,
        flops=2 * 48 * W**3, data=8 << 20, mb=49,
    )
    taken = lax.ppermute(give, ALL, SWAP)
    got = lax.ppermute(grad, ALL, back(SIDE))
    above_first = lax.ppermute(grad, ALL, back(UP))
    above_second = lax.ppermute(grad, ALL, back(SLANT))
    mine = (keep + taken).reshape(64, 16, W)
    inside = offsets[0, 0] >= 0
    parts = lax.cond(inside, exchange, jnp.zeros_like, mine)
    parts, got, above_first, above_second = lax.optimization_barrier((parts, got, above_first, above_second))
    copies = call(
        sum_kernel, [(64, 16, W)], [HBM], [(64, 16, W), (8, 16, W)], 12, parts, data=2 << 20, mb=50,
    )[0]
    mine = lax.all_to_all(copies, CHIPS, 0, 0, tiled=True)
    new_object = call(
        object_kernel, [(2, TILE, TILE)], [HBM, SMEM] + [HBM] * 5,
        [offs_buf, (2, TILE, TILE), PIECE, PIECE, PIECE, PIECE, (2, TILE, TILE)], 13,
        offsets, scale, object_field, grad, got, above_first, above_second, data=6 << 20,
    )[0]
    mine, new_object = lax.optimization_barrier((mine, new_object))
    mine = mine.reshape(half)
    theirs = lax.ppermute(mine, ALL, SWAP)
    new_probe = call(
        functools.partial(probe_kernel, True), [modes], [HBM] * 2, [half, half, half], 6,
        probe, mine, data=3 << 20, mb=50,
    )[0]
    new_probe = call(
        functools.partial(probe_kernel, False), [modes], [HBM] * 3, [half, half, half], 6,
        probe, theirs, new_probe, data=3 << 20, mb=50, alias=((2, 0),),
    )[0]
    return (new_object, new_probe)


def solution(mesh):
    inner = Mesh(mesh.devices.reshape(4, 2, 4, 4), ALL)
    tables = dft_tables()
    placed = (P(None, ("x", "core"), COL), P(), P(ALL, None, None), P(), P())

    def whole(*args):
        return shards(jnp.asarray(tables), *args)

    return jax.shard_map(
        whole, mesh=inner, in_specs=placed, out_specs=(P(None, ("x", "core"), COL), P()), check_vma=False
    )
```
